512 devices in a mesh: slot: 16 (over z), seq: 8 (over y_lo, x), head: 4 (over y_hi, core).
Axes of the slice: x: 4, y: 4 (y_hi: 2, y_lo: 2; y = y_hi * 2 + y_lo), z: 16, core: 2. Of those that a mesh axis runs over, the one named last changes fastest.
Arguments:
- hidden: bfloat16 [10240, 5120], P(('slot', 'seq'), 'head')
- final_mod: float32 [16, 2, 5120], P('slot', None, 'head'), may hold values from -3 to 3
- head_weight: float32 [5120, 64], P('head'), may hold values from -0.078125 to 0.078125
- latents: float32 [10240, 64], P(('slot', 'seq')), may hold values from -6 to 6
- fresh_noise: float32 [640, 64], P('seq'), may hold values from -6 to 6
- step_index: int32 [16], replicated, may hold values from 1 to 48, as said below
- slot_group: int32 [16], replicated, may hold values from 0 to 15, each once
- group_mask: int32 [16, 16], replicated, may hold values from 0 to 1, as said below
- patch_weight: bfloat16 [64, 5120], replicated, may hold values from -0.75 to 0.75
- block_mod: float32 [16, 2, 5120], P('slot'), may hold values from -3 to 3
- qkv_weight: bfloat16 [5120, 3, 4096], P(None, None, ('seq', 'head')), may hold values from -0.078125 to 0.078125
Outputs:
- stepped: float32 [10240, 64], P(('slot', 'seq'))
- attn_out: bfloat16 [10240, 4096], P('slot', ('seq', 'head'))
The draws below stay inside these ranges and needn't reach their ends.
Inputs may be any that keep to these rules, and one draw needn't show every extreme that they name: `step_index`: falls strictly from slot to slot; slot s lies in (16 - s - 1) * 3 + 1 to (16 - s) * 3, slot 0 at the top. `group_mask`: row i is 1 exactly on a run of groups that ends at group i, 0 elsewhere.
All inputs are finite; a program needn't handle non-finite values.
Results may differ from the reference program's by a relative error of at most 0.0049.
Values may be sent and summed in bfloat16 or wider, within the bound.
A program may use at most 64 MiB of HBM per device.

```python
import math
import jax
import jax.numpy as jnp
from jax import lax

D = 5120
HD = 128
PATCH = 64
HQ = 32
STEPS = 48
SLOTS = 16
GROUP = 640
TOKENS = 10240
WIDTH = 4096
GAP = 3


def draw_hidden(key, part):
    key = jax.random.fold_in(key, 11)
    keys_all = jax.random.split(key, 3)
    base = jax.random.normal(keys_all[0], (TOKENS, D), jnp.float32)
    column = jnp.arange(D, dtype=jnp.float32) / D
    column_scale = jnp.exp(jnp.log(3.0) * column + jax.random.uniform(keys_all[1], (D,), jnp.float32, -1.2, 1.2))
    row_scale = jnp.exp(jax.random.uniform(keys_all[2], (TOKENS, 1), jnp.float32, 0.0, 2.4))
    return (base * column_scale * row_scale * 0.5).astype(jnp.bfloat16)


def draw_step_index(key, part):
    key = jax.random.fold_in(key, 23)
    slot_ids = jnp.arange(SLOTS, dtype=jnp.int32)
    offsets = jax.random.randint(key, (SLOTS,), 0, GAP, dtype=jnp.int32)
    offsets = jnp.where(slot_ids == 0, 0, offsets)
    return ((SLOTS - slot_ids) * GAP - offsets).astype(jnp.int32)


def draw_group_mask(key, part):
    key = jax.random.fold_in(key, 37)
    reach = jax.random.randint(key, (SLOTS, 1), 0, SLOTS, dtype=jnp.int32)
    row_ids = jnp.arange(SLOTS, dtype=jnp.int32)[:, None]
    col_ids = jnp.arange(SLOTS, dtype=jnp.int32)[None, :]
    return ((col_ids <= row_ids) & (col_ids >= row_ids - reach)).astype(jnp.int32)


def block_levels(own_key, shape, cuts, low, high):
    level = 1.0
    for axis_at, parts in cuts:
        heights = jax.random.uniform(jax.random.fold_in(jax.random.fold_in(own_key, 6), axis_at), (parts,), jnp.float32, low / len(cuts), high / len(cuts))
        level = level * jnp.repeat(jnp.exp(heights), shape[axis_at] // parts).reshape((-1,) + (1,) * (len(shape) - 1 - axis_at))
    return level


def bell_draw(rng, extent, width, limit, shards=(), kind=jnp.bfloat16):
    values = jax.random.normal(rng, extent, jnp.float32) * width
    if len(shards) > 0:
        values = block_levels(rng, extent, shards, -0.22, 0.18) * values
    return jnp.clip(values, min=-limit, max=limit).astype(kind)


def setup_inputs(seed: int = 0) -> dict:
    key_of = jax.random.split(jax.random.key(seed), 12)
    hidden = draw_hidden(jax.random.fold_in(key_of[11], 71), 0)
    final_mod = bell_draw(key_of[1], (SLOTS, 2, D), 0.5, 3.0, ((0, 16), (2, 4)), jnp.float32)
    head_weight = bell_draw(key_of[2], (D, PATCH), D ** -0.5, 0.078125, ((0, 4),), jnp.float32)
    latents = bell_draw(key_of[3], (TOKENS, PATCH), 1.0, 6.0, ((0, 128),), jnp.float32)
    fresh_noise = bell_draw(key_of[4], (GROUP, PATCH), 1.0, 6.0, ((0, 8),), jnp.float32)
    step_index = draw_step_index(jax.random.fold_in(key_of[11], 71), 0)
    slot_group = jax.random.permutation(key_of[6], SLOTS).astype(jnp.int32)
    group_mask = draw_group_mask(jax.random.fold_in(key_of[11], 71), 0)
    patch_weight = bell_draw(key_of[8], (PATCH, D), PATCH ** -0.5, 0.75)
    block_mod = bell_draw(key_of[9], (SLOTS, 2, D), 0.5, 3.0, ((0, 16),), jnp.float32)
    qkv_weight = bell_draw(key_of[10], (D, 3, WIDTH), D ** -0.5, 0.078125, ((2, 32),))
    return {"hidden": hidden, "final_mod": final_mod, "head_weight": head_weight, "latents": latents, "fresh_noise": fresh_noise, "step_index": step_index, "slot_group": slot_group, "group_mask": group_mask, "patch_weight": patch_weight, "block_mod": block_mod, "qkv_weight": qkv_weight}


EPS_NORM = 1e-06

def sigma_of(levels):
    ratio = levels.astype(jnp.float32) / STEPS
    return 5.0 * ratio / (1.0 + 4.0 * ratio)

def layer_norm(matrix):
    row_mean = lax.optimization_barrier(jnp.mean(matrix, axis=-1, keepdims=True))
    centred = matrix - row_mean
    spread = lax.optimization_barrier(jnp.mean(centred * centred, axis=-1, keepdims=True))
    return centred * lax.rsqrt(spread + EPS_NORM)

def rms_heads(block):
    shaped = block.reshape(block.shape[0], -1, HD)
    return (shaped * lax.rsqrt(lax.optimization_barrier(jnp.mean(shaped * shaped, axis=-1, keepdims=True)) + EPS_NORM)).astype(jnp.bfloat16)

def reference(hidden, final_mod, head_weight, latents, fresh_noise, step_index, slot_group, group_mask, patch_weight, block_mod, qkv_weight):
    features = hidden.astype(jnp.float32).reshape(SLOTS, GROUP, D)
    final_normed = layer_norm(features) * (1.0 + final_mod[:, 0][:, None, :]) + final_mod[:, 1][:, None, :]
    velocity = jnp.einsum('scd,dp->scp', final_normed, head_weight, precision=lax.Precision.HIGHEST)
    sigma_now = sigma_of(step_index)
    sigma_next = sigma_of(jnp.concatenate([step_index[1:], jnp.zeros((1,), jnp.int32)]))
    stepped = latents.reshape(SLOTS, GROUP, PATCH) + (sigma_next - sigma_now)[:, None, None] * velocity
    shifted = jnp.concatenate([fresh_noise[None], stepped[:-1]], axis=0)
    flat_weight = qkv_weight.reshape(D, 3 * WIDTH)

    def project(inputs):
        rows_in, modulation = inputs
        embedded = jnp.dot(rows_in.astype(jnp.bfloat16), patch_weight, preferred_element_type=jnp.float32)
        mixed = (layer_norm(embedded) * (1.0 + modulation[0]) + modulation[1]).astype(jnp.bfloat16)
        projected = jnp.dot(mixed, flat_weight, preferred_element_type=jnp.float32).reshape(GROUP, 3, WIDTH)
        value_rows = projected[:, 2].reshape(GROUP, HQ, HD).astype(jnp.bfloat16)
        return (rms_heads(projected[:, 0]), rms_heads(projected[:, 1]), value_rows)
    queries, keys, values = lax.map(project, (shifted, block_mod))
    keys = keys.reshape(TOKENS, HQ, HD)
    values = values.reshape(TOKENS, HQ, HD)
    visible = group_mask[slot_group[:, None], slot_group[None, :]].astype(jnp.float32)

    def attend_slot(query_slot):
        keep_rows = jnp.repeat(visible[query_slot], GROUP)
        slot_queries = queries[query_slot]

        def attend_head(head_index):
            scores = jnp.dot(slot_queries[:, head_index], keys[:, head_index].T, preferred_element_type=jnp.float32) / math.sqrt(HD)
            weights = jnp.exp(scores) * keep_rows[None, :]
            probs = weights.astype(jnp.bfloat16)
            summed = jnp.dot(probs, values[:, head_index], preferred_element_type=jnp.float32)
            return (summed / lax.optimization_barrier(jnp.sum(weights, axis=1, keepdims=True))).astype(jnp.bfloat16)
        return lax.map(attend_head, jnp.arange(HQ))
    attended = lax.map(attend_slot, jnp.arange(SLOTS))
    attn_out = jnp.transpose(attended, (0, 2, 1, 3)).reshape(TOKENS, WIDTH)
    return (stepped.reshape(TOKENS, PATCH), attn_out)
```

```python
import functools
import math

import jax
import jax.numpy as jnp
from jax import lax
from jax.experimental import pallas as pl
from jax.experimental.pallas import tpu as pltpu
from jax.sharding import PartitionSpec as P

D = 5120
HD = 128
STEPS = 48
PATCH = 64
SLOTS = 16
SEQ = 8
HEADS = 4
TOK = 80
HALF = 40
XROWS = 48
MROWS = 16
FEAT = D // SEQ
EPS = 1e-06
MESH = pl.DeviceIdType.MESH
HIGHEST = lax.Precision.HIGHEST
F32 = jnp.float32
BF16 = jnp.bfloat16
NT = (((1,), (1,)), ((), ()))
NEAR_EVEN = (0, 2, 14, 4, 12, 6, 10, 8)
NEAR_ODD = (1, 15, 3, 13, 5, 11, 7, 9)


def remote(src, dst, send_sem, recv_sem, device_id):
    return pltpu.make_async_remote_copy(
        src_ref=src,
        dst_ref=dst,
        send_sem=send_sem,
        recv_sem=recv_sem,
        device_id=device_id,
        device_id_type=MESH,
    )


class Spread:
    def __init__(self, buf, zs, zr, qs, qr, cs, cr):
        self.buf = buf
        self.zs, self.zr, self.qs, self.qr, self.cs, self.cr = zs, zr, qs, qr, cs, cr
        self.slot = lax.axis_index("slot")
        self.seq = lax.axis_index("seq")
        self.head = lax.axis_index("head")
        self.core = lax.rem(self.head, 2)
        self.own = lax.rem(self.slot, 2) == self.core
        self.other_core = self.head + 1 - 2 * self.core

    def source(self, i, mine=True):
        near = jnp.where(self.own, NEAR_EVEN[i], NEAR_ODD[i]) if mine else jnp.where(
            self.own, NEAR_ODD[i], NEAR_EVEN[i]
        )
        return lax.rem(self.slot + near, SLOTS)

    def slot_copy(self, k):
        block = self.buf.at[self.slot, self.seq]
        return remote(
            block, block, self.zs.at[k], self.zr.at[self.slot], {"slot": lax.rem(self.slot + k, SLOTS)}
        )

    def slot_send(self):
        @pl.when(self.own)
        def _():
            @pl.loop(1, SLOTS)
            def _(k):
                self.slot_copy(k).start()

    def slot_wait(self, i):
        src = self.source(i)
        block = self.buf.at[src, self.seq]

        def wait():
            remote(block, block, self.zs.at[0], self.zr.at[src], {"slot": self.slot}).wait_recv()

        if i == 0:
            pl.when(jnp.logical_not(self.own))(wait)
        else:
            wait()

    def seq_send(self, i):
        src = self.source(i)
        block = self.buf.at[src, self.seq]

        @pl.loop(1, SEQ)
        def _(k):
            remote(
                block, block, self.qs.at[src], self.qr.at[src], {"seq": lax.rem(self.seq + k, SEQ)}
            ).start()

    def seq_all(self, src):
        blocks = self.buf.at[src, pl.ds(0, SEQ - 1)]
        return remote(blocks, blocks, self.qs.at[src], self.qr.at[src], {"seq": self.seq})

    def core_copy(self, src):
        blocks = self.buf.at[src]
        return remote(
            blocks, blocks, self.cs.at[src], self.cr.at[src], {"head": self.other_core}
        )

    def core_send(self, i):
        src = self.source(i)
        self.seq_all(src).wait_recv()
        self.core_copy(src).start()

    def core_wait(self, i):
        self.core_copy(self.source(i, mine=False)).wait_recv()

    def finish(self):
        @pl.when(self.own)
        def _():
            @pl.loop(1, SLOTS)
            def _(k):
                self.slot_copy(k).wait_send()

        for i in range(SLOTS // 2):
            src = self.source(i)
            self.seq_all(src).wait_send()
            self.core_copy(src).wait_send()


def partial_velocity(hidden, final_mod, head_t, msg):
    h = hidden[...].astype(F32)
    mean = jnp.mean(h, axis=1, keepdims=True)
    centred = h - mean
    spread = jnp.sum(centred * centred, axis=1, keepdims=True)
    weight = head_t[...] * (1.0 + final_mod[0, 0:1, :])
    part = lax.dot_general(centred, weight, NT, precision=HIGHEST, preferred_element_type=F32)
    ones = jnp.ones((8, weight.shape[1]), F32)
    gain_sum = lax.dot_general(ones, weight, NT, precision=HIGHEST, preferred_element_type=F32)
    shift = jnp.broadcast_to(final_mod[0, 1:2, :], ones.shape)
    shift_sum = lax.dot_general(shift, head_t[...], NT, precision=HIGHEST, preferred_element_type=F32)
    lane = lax.broadcasted_iota(jnp.int32, (TOK, PATCH), 1)
    stats = jnp.where(lane == 0, mean, jnp.where(lane == 1, spread, 0.0))
    msg[0:TOK, :] = jnp.concatenate([part, stats], axis=1)
    msg[TOK : TOK + 8, :] = jnp.concatenate([gain_sum, shift_sum], axis=1)


def whole_velocity(parts, count):
    means = [p[0:TOK, PATCH : PATCH + 1] for p in parts]
    mean = sum(means) / len(parts)
    spread = 0.0
    total = 0.0
    shift = 0.0
    for p, m in zip(parts, means):
        off = m - mean
        spread = spread + p[0:TOK, PATCH + 1 : PATCH + 2] + count * off * off
        total = total + p[0:TOK, 0:PATCH] + off * p[TOK : TOK + 1, 0:PATCH]
        shift = shift + p[TOK : TOK + 1, PATCH : 2 * PATCH]
    return total * lax.rsqrt(spread / (count * len(parts)) + EPS) + shift


def sigma_of(level):
    ratio = jnp.full((1, PATCH), level, jnp.int32).astype(F32) / STEPS
    return 5.0 * ratio / (1.0 + 4.0 * ratio)


def move_kernel(
    hidden,
    final_mod,
    head_t,
    latents_t,
    noise_t,
    step_index,
    patch_weight,
    block_mod,
    stepped_t,
    xall,
    mall,
    msg,
    got,
    ps,
    pr,
    *sems,
):
    x = Spread(xall, *sems[:6])
    m = Spread(mall, *sems[6:])
    slot, seq, head = x.slot, x.seq, x.head
    barrier = pltpu.get_barrier_semaphore()
    for axis, index, size in (("head", head, HEADS), ("seq", seq, SEQ), ("slot", slot, SLOTS)):
        for k in range(1, size):
            pl.semaphore_signal(
                barrier, inc=1, device_id={axis: lax.rem(index + k, size)}, device_id_type=MESH
            )
    partial_velocity(hidden, final_mod, head_t, msg)

    @pl.when(x.own)
    def _():
        start = pl.multiple_of(seq * FEAT, 128)
        both = block_mod[0, :, pl.ds(start, FEAT)]
        gain = 1.0 + both[0:1]
        rows = [gain[:, 128 * r : 128 * r + 128] for r in range(FEAT // 128)]
        rows += [jnp.zeros((3, 128), F32)]
        rows += [both[1:2, 128 * r : 128 * r + 128] for r in range(FEAT // 128)]
        rows += [jnp.zeros((3, 128), F32)]
        mall[slot, seq] = jnp.concatenate(rows, axis=0).astype(BF16)

    pl.semaphore_wait(barrier, HEADS + SEQ + SLOTS - 3)
    sends = [
        remote(msg, got.at[k - 1], ps.at[k - 1], pr.at[k - 1], {"head": lax.rem(head + k, HEADS)})
        for k in range(1, HEADS)
    ]
    for copy in sends:
        copy.start()
    m.slot_send()

    weight = patch_weight[...]
    gram = lax.dot_general(weight, weight, NT, preferred_element_type=F32) / D
    ones = jnp.ones((16, D), BF16)
    mean_row = lax.dot_general(ones, weight, NT, preferred_element_type=F32)[0:8] / D
    mean_outer = lax.dot_general(
        mean_row, mean_row, (((0,), (0,)), ((), ())), precision=HIGHEST, preferred_element_type=F32
    ) / 8.0
    gram = gram - mean_outer
    latents = jnp.transpose(latents_t[...])
    noise = jnp.transpose(noise_t[...])
    now = step_index[slot]
    later = jnp.where(slot == SLOTS - 1, 0, step_index[jnp.minimum(slot + 1, SLOTS - 1)])
    delta = sigma_of(later) - sigma_of(now)

    for copy in sends:
        copy.wait_recv()
    velocity = whole_velocity([msg[...]] + [got[k] for k in range(HEADS - 1)], D // HEADS)
    stepped = latents + delta * velocity
    shifted = jnp.where(slot == SLOTS - 1, noise, stepped).astype(BF16).astype(F32)
    projected = jnp.dot(shifted, gram, precision=HIGHEST, preferred_element_type=F32)
    spread = jnp.sum(projected * shifted, axis=1, keepdims=True)
    scaled = shifted * lax.rsqrt(jnp.maximum(spread, 0.0) + EPS)
    block = jnp.concatenate([scaled[0:HALF], scaled[HALF:TOK]], axis=1)
    block = jnp.concatenate([block, jnp.zeros((XROWS - HALF, 128), F32)], axis=0).astype(BF16)

    @pl.when(x.own)
    def _():
        xall[slot, seq] = block

    x.slot_send()
    stepped_t[...] = jnp.transpose(stepped)
    count = SLOTS // 2
    for i in range(count):
        m.slot_wait(i)
        m.seq_send(i)
    for i in range(count):
        x.slot_wait(i)
        x.seq_send(i)
        m.core_send(i)
    for i in range(count):
        x.core_send(i)
    for i in range(count):
        m.core_wait(i)
        x.core_wait(i)
    for copy in sends:
        copy.wait_send()
    m.finish()
    x.finish()


def attend_kernel(
    slot_group, group_mask, xall, mall, qkv, patch_weight, out, centred, lhs, a_kv, a_q, q_ref, total
):
    slot = lax.axis_index("slot")
    weight = patch_weight[...].astype(F32)
    centred[...] = weight - jnp.mean(weight, axis=1, keepdims=True)
    base = SLOTS * PATCH

    a_kv[...] = jnp.zeros_like(a_kv)
    a_q[...] = jnp.zeros_like(a_q)
    parts = FEAT // 128

    @pl.loop(0, SEQ)
    def _(p):
        start = pl.multiple_of(p * FEAT, 128)

        @pl.loop(0, SLOTS)
        def _(b):
            mods = mall[b, p].astype(F32)
            rows = pl.ds(pl.multiple_of(b * PATCH, PATCH), PATCH)
            for r in range(parts):
                piece = centred[:, pl.ds(pl.multiple_of(start + 128 * r, 128), 128)]
                lhs[rows, 128 * r : 128 * r + 128] = (piece * mods[r : r + 1]).astype(BF16)

        for r in range(parts):
            shifts = [mall[b, p].astype(F32)[8 + r : 9 + r] for b in range(SLOTS)]
            lhs[base : base + SLOTS, 128 * r : 128 * r + 128] = jnp.concatenate(shifts, axis=0).astype(BF16)
        depth = pl.ds(start, FEAT)
        a_kv[:, 0:HD] += jnp.dot(lhs[...], qkv[1, depth, :], preferred_element_type=F32)
        a_kv[:, HD : 2 * HD] += jnp.dot(lhs[...], qkv[2, depth, :], preferred_element_type=F32)
        own = lhs[pl.ds(pl.multiple_of(slot * PATCH, PATCH), PATCH), :]
        own = jnp.concatenate([own, lhs[base : base + SLOTS, :]], axis=0)
        a_q[...] += jnp.dot(own, qkv[0, depth, :], preferred_element_type=F32)

    def tokens(src, matrix, bias):
        blocks = xall[src].reshape(SEQ * XROWS, 128)
        zero = jnp.zeros_like(matrix)
        found = []
        for pair in ([matrix, zero], [zero, matrix]):
            wide = jnp.dot(blocks, jnp.concatenate(pair, axis=0), preferred_element_type=F32)
            wide = wide.reshape(SEQ, XROWS, wide.shape[1])[:, 0:HALF]
            found.append(wide.reshape(SEQ * HALF, wide.shape[2]) + bias)
        return found

    def unit(block):
        return block * lax.rsqrt(jnp.mean(block * block, axis=1, keepdims=True) + EPS)

    first, second = tokens(
        lax.rem(slot + SLOTS - 1, SLOTS), a_q[0:PATCH].astype(BF16), a_q[pl.ds(PATCH + slot, 1), :]
    )
    scale = 1.0 / (math.sqrt(HD) * math.log(2.0))
    group = SEQ * HALF
    for at, block in ((0, first), (1, second)):
        q_ref[at * group : at * group + group, :] = (unit(block) * scale).astype(BF16)
    total[...] = jnp.zeros_like(total)
    mine = slot_group[slot]

    @pl.loop(0, SLOTS)
    def _(b):
        @pl.when(group_mask[mine, slot_group[b]] != 0)
        def _():
            rows = pl.ds(pl.multiple_of(b * PATCH, PATCH), PATCH)
            pair = tokens(
                lax.rem(b + SLOTS - 1, SLOTS), a_kv[rows, :].astype(BF16), a_kv[pl.ds(base + b, 1), :]
            )
            keys = jnp.concatenate([unit(t[:, 0:HD]) for t in pair], axis=0).astype(BF16)
            values = jnp.concatenate([t[:, HD : 2 * HD] for t in pair], axis=0).astype(BF16)
            values = jnp.concatenate([values, jnp.ones_like(values)], axis=1)
            for at in range(5):
                part = slice(at * 128, at * 128 + 128)
                scores = lax.dot_general(q_ref[part, :], keys, NT, preferred_element_type=F32)
                probs = jnp.exp2(scores).astype(BF16)
                total[part, :] += jnp.dot(probs, values, preferred_element_type=F32)

    for p in range(SEQ):
        found = []
        for half in range(2):
            rows = slice(half * group + p * HALF, half * group + p * HALF + HALF)
            found.append(total[rows, 0:HD] / total[rows, HD : 2 * HD])
        out[p * TOK : p * TOK + TOK, :] = jnp.concatenate(found, axis=0).astype(out.dtype)


def spread_sems():
    dma = pltpu.SemaphoreType.DMA
    return [dma((SLOTS,)) for _ in range(6)]


def local(
    hidden,
    final_mod,
    head_weight,
    latents,
    fresh_noise,
    step_index,
    slot_group,
    group_mask,
    patch_weight,
    block_mod,
    qkv_weight,
):
    vmem = pl.BlockSpec(memory_space=pltpu.VMEM)
    smem = pl.BlockSpec(memory_space=pltpu.SMEM)
    dma = pltpu.SemaphoreType.DMA
    stepped_t, xall, mall = pl.pallas_call(
        move_kernel,
        out_shape=(
            jax.ShapeDtypeStruct((PATCH, TOK), F32),
            jax.ShapeDtypeStruct((SLOTS, SEQ, XROWS, 128), BF16),
            jax.ShapeDtypeStruct((SLOTS, SEQ, MROWS, 128), BF16),
        ),
        in_specs=[vmem] * 5 + [smem] + [vmem] * 2,
        out_specs=(vmem,) * 3,
        scratch_shapes=[
            pltpu.VMEM((TOK + 8, 128), F32),
            pltpu.VMEM((HEADS - 1, TOK + 8, 128), F32),
            dma((HEADS - 1,)),
            dma((HEADS - 1,)),
        ]
        + spread_sems()
        + spread_sems(),
        compiler_params=pltpu.CompilerParams(
            collective_id=0, has_side_effects=True, vmem_limit_bytes=32 * 2**20
        ),
        name="move",
    )(
        hidden,
        final_mod,
        head_weight.T,
        latents.T,
        fresh_noise.T,
        step_index,
        patch_weight,
        block_mod,
    )
    rows = SLOTS * PATCH + SLOTS
    attn = pl.pallas_call(
        attend_kernel,
        out_shape=jax.ShapeDtypeStruct((SEQ * TOK, HD), BF16),
        in_specs=[smem] * 2 + [vmem] * 4,
        out_specs=vmem,
        scratch_shapes=[
            pltpu.VMEM((PATCH, D), F32),
            pltpu.VMEM((rows, FEAT), BF16),
            pltpu.VMEM((rows, 2 * HD), F32),
            pltpu.VMEM((PATCH + SLOTS, HD), F32),
            pltpu.VMEM((SEQ * TOK, HD), BF16),
            pltpu.VMEM((SEQ * TOK, 2 * HD), F32),
        ],
        compiler_params=pltpu.CompilerParams(vmem_limit_bytes=48 * 2**20),
        name="attend",
    )(slot_group, group_mask, xall, mall, jnp.transpose(qkv_weight, (1, 0, 2)), patch_weight)
    return stepped_t.T, attn


def solution(mesh):
    in_specs = (
        P(("slot", "seq"), "head"),
        P("slot", None, "head"),
        P("head", None),
        P(("slot", "seq"), None),
        P("seq", None),
        P(),
        P(),
        P(),
        P(),
        P("slot", None, None),
        P(None, None, ("seq", "head")),
    )
    out_specs = (P(("slot", "seq"), None), P("slot", ("seq", "head")))
    return jax.shard_map(local, mesh=mesh, in_specs=in_specs, out_specs=out_specs, check_vma=False)
```

```python
import math

import jax
import jax.numpy as jnp
from jax import lax
from jax.experimental import pallas as pl
from jax.experimental.pallas import tpu as pltpu
from jax.sharding import PartitionSpec as P

D = 5120
HD = 128
STEPS = 48
PATCH = 64
SLOTS = 16
SEQ = 8
HEADS = 4
CHUNKS = D // 128
TOK = 80
HALF = 40
XROWS = 48
MROWS = 16
FEAT = D // SEQ
EPS = 1e-06
MESH = pl.DeviceIdType.MESH
HIGHEST = lax.Precision.HIGHEST
F32 = jnp.float32
BF16 = jnp.bfloat16
NT = (((1,), (1,)), ((), ()))
PAIRS = SLOTS // 2
ROW = SEQ // 2
PARTS = FEAT // 128
KEYS = 2 * SEQ * TOK


def remote(src, dst, send_sem, recv_sem, device_id):
    return pltpu.make_async_remote_copy(
        src_ref=src,
        dst_ref=dst,
        send_sem=send_sem,
        recv_sem=recv_sem,
        device_id=device_id,
        device_id_type=MESH,
    )


class Spread:
    def __init__(self, buf, shift, sems):
        self.buf = buf
        self.zs, self.zr, self.qs, self.qr, self.ys, self.yr, self.cs, self.cr = sems
        self.shift = shift
        self.slot = lax.axis_index("slot")
        self.seq = lax.axis_index("seq")
        self.head = lax.axis_index("head")
        self.core = lax.rem(self.head, 2)
        self.own = lax.rem(self.slot, 2) == self.core
        self.other_core = self.head + 1 - 2 * self.core
        self.low = self.seq // ROW
        self.at = lax.rem(self.seq, ROW)

    def source(self, i, mine=True):
        odd = lax.rem(i, 2) == 1
        even_list = jnp.where(odd, i + 1, SLOTS - i)
        odd_list = jnp.where(odd, SLOTS - i, i + 1)
        if self.shift:
            even_list, odd_list = odd_list + 1, even_list + 1
        near = jnp.where(self.own, even_list, odd_list) if mine else jnp.where(self.own, odd_list, even_list)
        return lax.rem(self.slot + near, SLOTS)

    def half(self, src, low):
        return self.buf.at[src, pl.ds(low * ROW, ROW)]

    def slot_copy(self, k):
        block = self.buf.at[self.slot, self.seq]
        return remote(
            block, block, self.zs.at[k], self.zr.at[self.slot], {"slot": lax.rem(self.slot + k, SLOTS)}
        )

    def slot_send(self):
        @pl.when(self.own)
        def _():
            @pl.loop(1, SLOTS)
            def _(k):
                self.slot_copy(k).start()

    def slot_wait(self, i):
        src = self.source(i)
        block = self.buf.at[src, self.seq]

        @pl.when(src != self.slot)
        def _():
            remote(block, block, self.zs.at[0], self.zr.at[src], {"slot": self.slot}).wait_recv()

    def row_send(self, i):
        src = self.source(i)
        block = self.buf.at[src, self.seq]
        for k in range(1, ROW):
            to = self.low * ROW + lax.rem(self.at + k, ROW)
            remote(block, block, self.qs.at[src], self.qr.at[src], {"seq": to}).start()

    def row_all(self, src):
        blocks = self.buf.at[src, pl.ds(0, ROW - 1)]
        return remote(blocks, blocks, self.qs.at[src], self.qr.at[src], {"seq": self.seq})

    def side_copy(self, i):
        src = self.source(i)
        blocks = self.half(src, self.low)
        head = lax.rem(self.head + 2 * lax.rem(i, 2), HEADS)
        seq = (1 - self.low) * ROW + self.at
        return remote(blocks, blocks, self.ys.at[src], self.yr.at[src], {"seq": seq, "head": head})

    def core_copy(self, src, low):
        blocks = self.half(src, low)
        return remote(blocks, blocks, self.cs.at[src], self.cr.at[src], {"head": self.other_core})

    def core_all(self, src):
        blocks = self.buf.at[src]
        return remote(blocks, blocks, self.cs.at[src], self.cr.at[src], {"head": self.other_core})

    def first(self, i):
        self.slot_wait(i)
        self.row_send(i)

    def second(self, i):
        src = self.source(i)
        self.row_all(src).wait_recv()
        self.side_copy(i).start()
        self.core_copy(src, self.low).start()

    def third(self, i):
        src = self.source(i)
        self.side_copy(i).wait_recv()
        self.core_copy(src, 1 - self.low).start()

    def fourth(self, i):
        self.core_all(self.source(i, mine=False)).wait_recv()

    def finish(self):
        @pl.when(self.own)
        def _():
            @pl.loop(1, SLOTS)
            def _(k):
                self.slot_copy(k).wait_send()

        @pl.loop(0, PAIRS)
        def _(i):
            src = self.source(i)
            self.row_all(src).wait_send()
            self.side_copy(i).wait_send()
            self.core_all(src).wait_send()


def split(value, count):
    found = []
    for _ in range(count):
        part = value.astype(BF16)
        found.append(part)
        value = value - part.astype(F32)
    return found


def partial_velocity(hidden, final_mod, head_t, msg):
    h = hidden[...]
    wide = h.astype(F32)
    mean = jnp.mean(wide, axis=1, keepdims=True)
    centred = wide - mean
    spread = jnp.sum(centred * centred, axis=1, keepdims=True)
    gained = head_t[...] * (1.0 + final_mod[0, 0:1, :])
    gain_sum = jnp.sum(gained, axis=1, keepdims=True)
    shift_sum = jnp.sum(head_t[...] * final_mod[0, 1:2, :], axis=1, keepdims=True)
    stack = jnp.concatenate(split(gained, 3), axis=0)
    parts = lax.dot_general(h, stack, NT, preferred_element_type=F32)
    part = parts[:, 0:PATCH] + parts[:, PATCH : 2 * PATCH] + parts[:, 2 * PATCH : 3 * PATCH]
    lane = lax.broadcasted_iota(jnp.int32, (TOK, PATCH), 1)
    pad = jnp.zeros((TOK - PATCH, 1), F32)
    gain_sum = jnp.concatenate([gain_sum, pad], axis=0)
    shift_sum = jnp.concatenate([shift_sum, pad], axis=0)
    stats = jnp.where(lane == 0, mean, jnp.where(lane == 1, spread, 0.0))
    stats = jnp.where(lane == 2, gain_sum, jnp.where(lane == 3, shift_sum, stats))
    msg[...] = jnp.concatenate([part, stats], axis=1)


def whole_velocity(parts, count):
    total = sum(parts)
    mean = total[:, PATCH : PATCH + 1] / len(parts)
    spread = total[:, PATCH + 1 : PATCH + 2]
    for p in parts:
        off = p[:, PATCH : PATCH + 1] - mean
        spread = spread + count * off * off
    turned = jnp.transpose(jnp.concatenate([total, jnp.zeros((128 - TOK, 128), F32)], axis=0))
    gain_row = turned[PATCH + 2 : PATCH + 3, 0:PATCH]
    shift_row = turned[PATCH + 3 : PATCH + 4, 0:PATCH]
    scale = lax.rsqrt(spread / (count * len(parts)) + EPS)
    return (total[:, 0:PATCH] - mean * gain_row) * scale + shift_row


def sigma_of(level):
    ratio = jnp.full((1, PATCH), level, jnp.int32).astype(F32) / STEPS
    return 5.0 * ratio / (1.0 + 4.0 * ratio)


def unit(block):
    return block * lax.rsqrt(jnp.mean(block * block, axis=1, keepdims=True) + EPS)


def kernel(
    hidden_in,
    final_mod_in,
    head_in,
    latents_in,
    noise_in,
    step_in,
    group_in,
    mask_in,
    patch_in,
    block_in,
    qkv_in,
    stepped_out,
    attn_out,
    hidden,
    final_mod,
    head_t,
    latents_t,
    noise_t,
    step_index,
    slot_group,
    group_mask,
    patch_weight,
    block_mod,
    q_weight,
    kv_weight,
    stepped_t,
    attn,
    xall,
    mall,
    msg,
    got,
    centred,
    lhs,
    a_kv,
    b_kv,
    q_ref,
    keys,
    values,
    total,
    local_sem,
    ps,
    pr,
    *sems,
):
    x = Spread(xall, 0, sems[:8])
    m = Spread(mall, 1, sems[8:])
    slot, seq, head = x.slot, x.seq, x.head
    loads = [
        pltpu.make_async_copy(src, dst, local_sem.at[i])
        for i, (src, dst) in enumerate(
            (
                (hidden_in, hidden),
                (final_mod_in, final_mod),
                (head_in, head_t),
                (block_in, block_mod),
                (patch_in, patch_weight),
                (latents_in, latents_t),
                (noise_in, noise_t),
                (step_in, step_index),
                (group_in, slot_group),
                (mask_in, group_mask),
                (qkv_in.at[0], q_weight),
                (qkv_in.at[1], kv_weight.at[:, 0:HD]),
                (qkv_in.at[2], kv_weight.at[:, HD : 2 * HD]),
            )
        )
    ]
    for copy in loads:
        copy.start()
    barrier = pltpu.get_barrier_semaphore()

    def greet(device_id):
        pl.semaphore_signal(barrier, inc=1, device_id=device_id, device_id_type=MESH)

    for k in range(1, SLOTS):
        greet({"slot": lax.rem(slot + k, SLOTS)})
    for k in range(1, HEADS):
        greet({"head": lax.rem(head + k, HEADS)})
    for k in range(1, ROW):
        greet({"seq": x.low * ROW + lax.rem(x.at + k, ROW)})
    side = (1 - x.low) * ROW + x.at
    greet({"seq": side})
    greet({"seq": side, "head": lax.rem(head + 2, HEADS)})

    for copy in loads[:4]:
        copy.wait()
    partial_velocity(hidden, final_mod, head_t, msg)
    sub = lax.broadcasted_iota(jnp.int32, (MROWS, 128), 0)

    @pl.when(x.own)
    def _():
        start = pl.multiple_of(seq * FEAT, 128)
        gain = 1.0 + block_mod[0, 0:1, pl.ds(start, FEAT)]
        high, low = split(block_mod[0, 1:2, pl.ds(start, FEAT)], 2)
        rows = []
        for row in (gain, high.astype(F32), low.astype(F32)):
            rows += [row[:, 128 * r : 128 * r + 128] for r in range(PARTS)]
        rows += [jnp.zeros((1, 128), F32)]
        mall[slot, seq] = jnp.concatenate(rows, axis=0).astype(BF16)

    pl.semaphore_wait(barrier, SLOTS + HEADS + ROW - 3 + 2)
    sends = [
        remote(msg, got.at[k - 1], ps.at[k - 1], pr.at[k - 1], {"head": lax.rem(head + k, HEADS)})
        for k in range(1, HEADS)
    ]
    for copy in sends:
        copy.start()
    m.slot_send()

    for copy in loads[4:]:
        copy.wait()
    weight = patch_weight[...]
    gram = lax.dot_general(weight, weight, NT, preferred_element_type=F32) / D
    ones = jnp.ones((16, D), BF16)
    mean_row = lax.dot_general(ones, weight, NT, preferred_element_type=F32)[0:8] / D
    mean_outer = lax.dot_general(
        mean_row, mean_row, (((0,), (0,)), ((), ())), precision=HIGHEST, preferred_element_type=F32
    ) / 8.0
    gram = gram - mean_outer
    latents = jnp.transpose(latents_t[...])
    noise = jnp.transpose(noise_t[...])
    now = step_index[slot]
    later = jnp.where(slot == SLOTS - 1, 0, step_index[jnp.minimum(slot + 1, SLOTS - 1)])
    delta = sigma_of(later) - sigma_of(now)

    for copy in sends:
        copy.wait_recv()
    velocity = whole_velocity([msg[...]] + [got[k] for k in range(HEADS - 1)], D // HEADS)
    stepped = latents + delta * velocity
    shifted = jnp.where(slot == SLOTS - 1, noise, stepped).astype(BF16).astype(F32)
    projected = jnp.dot(shifted, gram, precision=HIGHEST, preferred_element_type=F32)
    spread = jnp.sum(projected * shifted, axis=1, keepdims=True)
    scaled = shifted * lax.rsqrt(jnp.maximum(spread, 0.0) + EPS)
    block = jnp.concatenate([scaled[0:HALF], scaled[HALF:TOK]], axis=1)
    block = jnp.concatenate([block, jnp.zeros((XROWS - HALF, 128), F32)], axis=0).astype(BF16)

    @pl.when(x.own)
    def _():
        xall[slot, seq] = block

    x.slot_send()
    stepped_t[...] = jnp.transpose(stepped)
    stepped_copy = pltpu.make_async_copy(stepped_t, stepped_out, local_sem.at[0])
    stepped_copy.start()

    wide = weight.astype(F32)
    centred[...] = wide - jnp.mean(wide, axis=1, keepdims=True)
    own_rows = PATCH + MROWS
    for c in range(CHUNKS):
        lanes = slice(128 * c, 128 * c + 128)
        gain = 1.0 + block_mod[0, 0:1, lanes]
        high, low = split(block_mod[0, 1:2, lanes], 2)
        lhs[0:PATCH, lanes] = (centred[:, lanes] * gain).astype(BF16)
        shifts = jnp.where(sub == 0, high.astype(F32), jnp.where(sub == 1, low.astype(F32), 0.0))
        lhs[PATCH:own_rows, lanes] = shifts.astype(BF16)
    found = jnp.dot(lhs[0:own_rows, :], q_weight[...], preferred_element_type=F32)
    a_q = found[0:PATCH]
    b_q = jnp.sum(found[PATCH:own_rows], axis=0, keepdims=True)

    def build(k):
        sources = [m.source(2 * k + e, mine) for e in range(2) for mine in (True, False)]

        for at, src in enumerate(sources):
            first = at * own_rows

            @pl.loop(0, SEQ)
            def _(p):
                mods = mall[src, p].astype(F32)
                for r in range(PARTS):
                    lanes = pl.ds(pl.multiple_of(p * FEAT + 128 * r, 128), 128)
                    lhs[first : first + PATCH, lanes] = (centred[:, lanes] * mods[r : r + 1]).astype(BF16)
                    kept = jnp.where((sub == PARTS + r) | (sub == 2 * PARTS + r), mods, 0.0)
                    lhs[first + PATCH : first + own_rows, lanes] = kept.astype(BF16)

        found = jnp.dot(lhs[...], kv_weight[...], preferred_element_type=F32)
        for at, src in enumerate(sources):
            first = at * own_rows
            a_kv[src] = found[first : first + PATCH].astype(BF16)
            b_kv[src] = jnp.broadcast_to(
                jnp.sum(found[first + PATCH : first + own_rows], axis=0, keepdims=True), (8, 2 * HD)
            )

    def tokens(src, matrix, bias):
        blocks = xall[src].reshape(SEQ * XROWS, 128)
        zero = jnp.zeros_like(matrix)
        found = []
        for pair in ([matrix, zero], [zero, matrix]):
            wide = jnp.dot(blocks, jnp.concatenate(pair, axis=0), preferred_element_type=F32)
            wide = wide.reshape(SEQ, XROWS, wide.shape[1])[:, 0:HALF]
            found.append(wide.reshape(SEQ * HALF, wide.shape[2]) + bias)
        return found

    group = SEQ * HALF
    mine = slot_group[slot]

    def prepare(i):
        for at, own in enumerate((True, False)):
            src = x.source(i, own)
            b = lax.rem(src + 1, SLOTS)
            keep = jnp.full((1, HD), group_mask[mine, slot_group[b]], jnp.int32).astype(F32)
            for half, t in enumerate(tokens(src, a_kv[b], b_kv[b][0:1])):
                rows = slice((2 * at + half) * group, (2 * at + half + 1) * group)
                keys[rows, :] = unit(t[:, 0:HD]).astype(BF16)
                values[rows, 0:HD] = (t[:, HD : 2 * HD] * keep).astype(BF16)
                values[rows, HD : 2 * HD] = jnp.broadcast_to(keep, (group, HD)).astype(BF16)

    def attend(i):
        prepare(i)
        scores = lax.dot_general(q_ref[...], keys[...], NT, preferred_element_type=F32)
        probs = jnp.exp2(scores).astype(BF16)
        total[...] += jnp.dot(probs, values[...], preferred_element_type=F32)

    total[...] = jnp.zeros_like(total)
    for i in range(PAIRS):
        m.first(i)
    for i in range(2):
        x.first(i)
    for i in range(4):
        m.second(i)
    for i in range(2, 4):
        x.first(i)
    for i in range(4, 8):
        m.second(i)
    for i in range(4, 6):
        x.first(i)
    for i in range(2):
        x.second(i)
    for i in range(8):
        m.third(i)
    for i in range(6, 8):
        x.first(i)
    for i in range(2, 4):
        x.second(i)
    for i in range(8):
        m.fourth(i)

    @pl.loop(0, PAIRS // 2)
    def _(k):
        build(k)

    for i in range(2):
        x.third(i)
    for i in range(4, 8):
        x.second(i)
    for i in range(2, 8):
        x.third(i)
    for i in range(2):
        x.fourth(i)
    scale = 1.0 / (math.sqrt(HD) * math.log(2.0))
    for half, t in enumerate(tokens(lax.rem(slot + SLOTS - 1, SLOTS), a_q.astype(BF16), b_q)):
        q_ref[half * group : half * group + group, :] = (unit(t) * scale).astype(BF16)

    @pl.loop(0, PAIRS)
    def _(i):
        @pl.when(i >= 2)
        def _():
            x.fourth(i)

        attend(i)

    for p in range(SEQ):
        found = []
        for half in range(2):
            rows = slice(half * group + p * HALF, half * group + p * HALF + HALF)
            found.append(total[rows, 0:HD] / total[rows, HD : 2 * HD])
        attn[p * TOK : p * TOK + TOK, :] = jnp.concatenate(found, axis=0).astype(attn.dtype)
    attn_copy = pltpu.make_async_copy(attn, attn_out, local_sem.at[1])
    attn_copy.start()
    for copy in sends:
        copy.wait_send()
    m.finish()
    x.finish()
    stepped_copy.wait()
    attn_copy.wait()


def spread_sems():
    dma = pltpu.SemaphoreType.DMA
    return [dma((SLOTS,)) for _ in range(8)]


def local(
    hidden,
    final_mod,
    head_weight,
    latents,
    fresh_noise,
    step_index,
    slot_group,
    group_mask,
    patch_weight,
    block_mod,
    qkv_weight,
):
    hbm = pl.BlockSpec(memory_space=pl.ANY)
    dma = pltpu.SemaphoreType.DMA
    vmem = pltpu.VMEM
    smem = pltpu.SMEM
    stepped_t, attn = pl.pallas_call(
        kernel,
        out_shape=(
            jax.ShapeDtypeStruct((PATCH, TOK), F32),
            jax.ShapeDtypeStruct((SEQ * TOK, HD), BF16),
        ),
        in_specs=[hbm] * 11,
        out_specs=(hbm, hbm),
        scratch_shapes=[
            vmem((TOK, D // HEADS), BF16),
            vmem((1, 2, D // HEADS), F32),
            vmem((PATCH, D // HEADS), F32),
            vmem((PATCH, TOK), F32),
            vmem((PATCH, TOK), F32),
            smem((SLOTS,), jnp.int32),
            smem((SLOTS,), jnp.int32),
            smem((SLOTS, SLOTS), jnp.int32),
            vmem((PATCH, D), BF16),
            vmem((1, 2, D), F32),
            vmem((D, HD), BF16),
            vmem((D, 2 * HD), BF16),
            vmem((PATCH, TOK), F32),
            vmem((SEQ * TOK, HD), BF16),
            vmem((SLOTS, SEQ, XROWS, 128), BF16),
            vmem((SLOTS, SEQ, MROWS, 128), BF16),
            vmem((TOK, 128), F32),
            vmem((HEADS - 1, TOK, 128), F32),
            vmem((PATCH, D), F32),
            vmem((4 * (PATCH + MROWS), D), BF16),
            vmem((SLOTS, PATCH, 2 * HD), BF16),
            vmem((SLOTS, 8, 2 * HD), F32),
            vmem((SEQ * TOK, HD), BF16),
            vmem((KEYS, HD), BF16),
            vmem((KEYS, 2 * HD), BF16),
            vmem((SEQ * TOK, 2 * HD), F32),
            dma((13,)),
            dma((HEADS - 1,)),
            dma((HEADS - 1,)),
        ]
        + spread_sems()
        + spread_sems(),
        compiler_params=pltpu.CompilerParams(
            collective_id=0, has_side_effects=True, vmem_limit_bytes=56 * 2**20
        ),
        name="window",
    )(
        hidden,
        final_mod,
        head_weight.T,
        latents.T,
        fresh_noise.T,
        step_index,
        slot_group,
        group_mask,
        patch_weight,
        block_mod,
        jnp.transpose(qkv_weight, (1, 0, 2)),
    )
    return stepped_t.T, attn


def solution(mesh):
    in_specs = (
        P(("slot", "seq"), "head"),
        P("slot", None, "head"),
        P("head", None),
        P(("slot", "seq"), None),
        P("seq", None),
        P(),
        P(),
        P(),
        P(),
        P("slot", None, None),
        P(None, None, ("seq", "head")),
    )
    out_specs = (P(("slot", "seq"), None), P("slot", ("seq", "head")))
    return jax.shard_map(local, mesh=mesh, in_specs=in_specs, out_specs=out_specs, check_vma=False)
```

```python
import math

import jax
import jax.numpy as jnp
from jax import lax
from jax.experimental import pallas as pl
from jax.experimental.pallas import tpu as pltpu
from jax.sharding import PartitionSpec as P

D = 5120
HD = 128
STEPS = 48
PATCH = 64
SLOTS = 16
SEQ = 8
HEADS = 4
CHUNKS = D // 128
TOK = 80
HALF = 40
XROWS = 48
MROWS = 16
FEAT = D // SEQ
EPS = 1e-06
MESH = pl.DeviceIdType.MESH
HIGHEST = lax.Precision.HIGHEST
F32 = jnp.float32
BF16 = jnp.bfloat16
NT = (((1,), (1,)), ((), ()))
PAIRS = SLOTS // 2
ROW = SEQ // 2
PARTS = FEAT // 128
KEYS = 2 * SEQ * TOK


def remote(src, dst, send_sem, recv_sem, device_id):
    return pltpu.make_async_remote_copy(
        src_ref=src,
        dst_ref=dst,
        send_sem=send_sem,
        recv_sem=recv_sem,
        device_id=device_id,
        device_id_type=MESH,
    )


class Spread:
    def __init__(self, buf, shift, sems):
        self.buf = buf
        self.zs, self.zr, self.qs, self.qr, self.ys, self.yr, self.cs, self.cr = sems
        self.shift = shift
        self.slot = lax.axis_index("slot")
        self.seq = lax.axis_index("seq")
        self.head = lax.axis_index("head")
        self.core = lax.rem(self.head, 2)
        self.own = lax.rem(self.slot, 2) == self.core
        self.other_core = self.head + 1 - 2 * self.core
        self.low = self.seq // ROW
        self.at = lax.rem(self.seq, ROW)

    def source(self, i, mine=True):
        odd = lax.rem(i, 2) == 1
        even_list = jnp.where(odd, i + 1, SLOTS - i)
        odd_list = jnp.where(odd, SLOTS - i, i + 1)
        if self.shift:
            even_list, odd_list = odd_list + 1, even_list + 1
        near = jnp.where(self.own, even_list, odd_list) if mine else jnp.where(self.own, odd_list, even_list)
        return lax.rem(self.slot + near, SLOTS)

    def half(self, src, low):
        return self.buf.at[src, pl.ds(low * ROW, ROW)]

    def slot_copy(self, k):
        block = self.buf.at[self.slot, self.seq]
        return remote(
            block, block, self.zs.at[k], self.zr.at[self.slot], {"slot": lax.rem(self.slot + k, SLOTS)}
        )

    def slot_send(self):
        @pl.when(self.own)
        def _():
            for k in range(1, SLOTS):
                self.slot_copy(k // 2 if k % 2 == 0 else SLOTS - (k + 1) // 2).start()

    def slot_wait(self, i):
        src = self.source(i)
        block = self.buf.at[src, self.seq]

        @pl.when(src != self.slot)
        def _():
            remote(block, block, self.zs.at[0], self.zr.at[src], {"slot": self.slot}).wait_recv()

    def row_send(self, i):
        src = self.source(i)
        block = self.buf.at[src, self.seq]
        for k in range(1, ROW):
            to = self.low * ROW + lax.rem(self.at + k, ROW)
            remote(block, block, self.qs.at[src], self.qr.at[src], {"seq": to}).start()

    def row_all(self, src):
        blocks = self.buf.at[src, pl.ds(0, ROW - 1)]
        return remote(blocks, blocks, self.qs.at[src], self.qr.at[src], {"seq": self.seq})

    def side_copy(self, i):
        src = self.source(i)
        blocks = self.half(src, self.low)
        head = lax.rem(self.head + 2 * lax.rem(i, 2), HEADS)
        seq = (1 - self.low) * ROW + self.at
        return remote(blocks, blocks, self.ys.at[src], self.yr.at[src], {"seq": seq, "head": head})

    def core_copy(self, src, low):
        blocks = self.half(src, low)
        return remote(blocks, blocks, self.cs.at[src], self.cr.at[src], {"head": self.other_core})

    def core_all(self, src):
        blocks = self.buf.at[src]
        return remote(blocks, blocks, self.cs.at[src], self.cr.at[src], {"head": self.other_core})

    def first(self, i):
        self.slot_wait(i)
        self.row_send(i)

    def second(self, i):
        src = self.source(i)
        self.row_all(src).wait_recv()
        self.side_copy(i).start()
        self.core_copy(src, self.low).start()

    def third(self, i):
        src = self.source(i)
        self.side_copy(i).wait_recv()
        self.core_copy(src, 1 - self.low).start()

    def fourth(self, i):
        self.core_all(self.source(i, mine=False)).wait_recv()

    def finish(self):
        @pl.when(self.own)
        def _():
            @pl.loop(1, SLOTS)
            def _(k):
                self.slot_copy(k).wait_send()

        @pl.loop(0, PAIRS)
        def _(i):
            src = self.source(i)
            self.row_all(src).wait_send()
            self.side_copy(i).wait_send()
            self.core_all(src).wait_send()


def split(value, count):
    found = []
    for _ in range(count):
        part = value.astype(BF16)
        found.append(part)
        value = value - part.astype(F32)
    return found


def partial_velocity(hidden, final_mod, head_t, msg):
    h = hidden[...]
    wide = h.astype(F32)
    mean = jnp.mean(wide, axis=1, keepdims=True)
    centred = wide - mean
    spread = jnp.sum(centred * centred, axis=1, keepdims=True)
    gained = head_t[...] * (1.0 + final_mod[0, 0:1, :])
    gain_sum = jnp.sum(gained, axis=1, keepdims=True)
    shift_sum = jnp.sum(head_t[...] * final_mod[0, 1:2, :], axis=1, keepdims=True)
    stack = jnp.concatenate(split(gained, 3), axis=0)
    parts = lax.dot_general(h, stack, NT, preferred_element_type=F32)
    part = parts[:, 0:PATCH] + parts[:, PATCH : 2 * PATCH] + parts[:, 2 * PATCH : 3 * PATCH]
    lane = lax.broadcasted_iota(jnp.int32, (TOK, 128), 1)
    pad = jnp.zeros((TOK - PATCH, 1), F32)
    gain_sum = jnp.concatenate([gain_sum, pad], axis=0)
    shift_sum = jnp.concatenate([shift_sum, pad], axis=0)
    stats = jnp.where(lane == 0, mean, jnp.where(lane == 1, spread, 0.0))
    stats = jnp.where(lane == 2, gain_sum, jnp.where(lane == 3, shift_sum, stats))
    stats = jnp.transpose(jnp.concatenate([stats, jnp.zeros((128 - TOK, 128), F32)], axis=0))
    msg[0:HALF, :] = jnp.concatenate([part[0:HALF], part[HALF:TOK]], axis=1)
    msg[HALF:XROWS, :] = stats[0:8]


def whole_velocity(parts, count):
    total = sum(parts)
    mean = total[HALF : HALF + 1] / len(parts)
    spread = total[HALF + 1 : HALF + 2]
    for p in parts:
        off = p[HALF : HALF + 1] - mean
        spread = spread + count * off * off
    scale = lax.rsqrt(spread / (count * len(parts)) + EPS)
    turned = jnp.transpose(jnp.concatenate([mean, scale, jnp.zeros((126, 128), F32)], axis=0))[0:TOK]
    gain_row = total[HALF + 2 : HALF + 3, 0:PATCH]
    shift_row = total[HALF + 3 : HALF + 4, 0:PATCH]
    product = jnp.concatenate([total[0:HALF, 0:PATCH], total[0:HALF, PATCH:128]], axis=0)
    return (product - turned[:, 0:1] * gain_row) * turned[:, 1:2] + shift_row


def sigma_of(level):
    ratio = jnp.full((1, PATCH), level, jnp.int32).astype(F32) / STEPS
    return 5.0 * ratio / (1.0 + 4.0 * ratio)


def unit(block):
    return block * lax.rsqrt(jnp.mean(block * block, axis=1, keepdims=True) + EPS)


def kernel(
    hidden_in,
    final_mod_in,
    head_in,
    latents_in,
    noise_in,
    step_in,
    group_in,
    mask_in,
    patch_in,
    block_in,
    qkv_in,
    stepped_out,
    attn_out,
    hidden,
    final_mod,
    head_t,
    latents_t,
    noise_t,
    step_index,
    slot_group,
    group_mask,
    patch_weight,
    block_mod,
    q_weight,
    kv_weight,
    stepped_t,
    attn,
    xall,
    mall,
    msg,
    got,
    centred,
    lhs,
    a_kv,
    b_kv,
    q_ref,
    keys_a,
    values_a,
    keys_b,
    values_b,
    total,
    local_sem,
    ps,
    pr,
    *sems,
):
    x = Spread(xall, 0, sems[:8])
    m = Spread(mall, 1, sems[8:])
    slot, seq, head = x.slot, x.seq, x.head
    loads = [
        pltpu.make_async_copy(src, dst, local_sem.at[i])
        for i, (src, dst) in enumerate(
            (
                (hidden_in, hidden),
                (final_mod_in, final_mod),
                (head_in, head_t),
                (block_in, block_mod),
                (patch_in, patch_weight),
                (latents_in, latents_t),
                (noise_in, noise_t),
                (step_in, step_index),
                (group_in, slot_group),
                (mask_in, group_mask),
                (qkv_in.at[0], q_weight),
                (qkv_in.at[1], kv_weight.at[:, 0:HD]),
                (qkv_in.at[2], kv_weight.at[:, HD : 2 * HD]),
            )
        )
    ]
    for copy in loads:
        copy.start()
    barrier = pltpu.get_barrier_semaphore()

    def greet(device_id):
        pl.semaphore_signal(barrier, inc=1, device_id=device_id, device_id_type=MESH)

    for k in range(1, SLOTS):
        greet({"slot": lax.rem(slot + k, SLOTS)})
    for k in range(1, HEADS):
        greet({"head": lax.rem(head + k, HEADS)})
    for k in range(1, ROW):
        greet({"seq": x.low * ROW + lax.rem(x.at + k, ROW)})
    side = (1 - x.low) * ROW + x.at
    greet({"seq": side})
    greet({"seq": side, "head": lax.rem(head + 2, HEADS)})

    for copy in loads[:4]:
        copy.wait()
    partial_velocity(hidden, final_mod, head_t, msg)
    sub = lax.broadcasted_iota(jnp.int32, (MROWS, 128), 0)

    @pl.when(x.own)
    def _():
        start = pl.multiple_of(seq * FEAT, 128)
        gain = 1.0 + block_mod[0, 0:1, pl.ds(start, FEAT)]
        high, low = split(block_mod[0, 1:2, pl.ds(start, FEAT)], 2)
        rows = []
        for row in (gain, high.astype(F32), low.astype(F32)):
            rows += [row[:, 128 * r : 128 * r + 128] for r in range(PARTS)]
        rows += [jnp.zeros((1, 128), F32)]
        mall[slot, seq] = jnp.concatenate(rows, axis=0).astype(BF16)

    pl.semaphore_wait(barrier, SLOTS + HEADS + ROW - 3 + 2)
    sends = [
        remote(msg, got.at[k - 1], ps.at[k - 1], pr.at[k - 1], {"head": lax.rem(head + k, HEADS)})
        for k in range(1, HEADS)
    ]
    for copy in sends:
        copy.start()
    m.slot_send()

    for copy in loads[4:]:
        copy.wait()
    weight = patch_weight[...]
    gram = lax.dot_general(weight, weight, NT, preferred_element_type=F32) / D
    ones = jnp.ones((16, D), BF16)
    mean_row = lax.dot_general(ones, weight, NT, preferred_element_type=F32)[0:8] / D
    mean_outer = lax.dot_general(
        mean_row, mean_row, (((0,), (0,)), ((), ())), precision=HIGHEST, preferred_element_type=F32
    ) / 8.0
    gram = gram - mean_outer
    latents = jnp.transpose(latents_t[...])
    noise = jnp.transpose(noise_t[...])
    now = step_index[slot]
    later = jnp.where(slot == SLOTS - 1, 0, step_index[jnp.minimum(slot + 1, SLOTS - 1)])
    delta = sigma_of(later) - sigma_of(now)

    for copy in sends:
        copy.wait_recv()
    velocity = whole_velocity([msg[...]] + [got[k] for k in range(HEADS - 1)], D // HEADS)
    stepped = latents + delta * velocity
    shifted = jnp.where(slot == SLOTS - 1, noise, stepped).astype(BF16).astype(F32)
    projected = jnp.dot(shifted, gram, precision=HIGHEST, preferred_element_type=F32)
    spread = jnp.sum(projected * shifted, axis=1, keepdims=True)
    scaled = shifted * lax.rsqrt(jnp.maximum(spread, 0.0) + EPS)
    block = jnp.concatenate([scaled[0:HALF], scaled[HALF:TOK]], axis=1)
    block = jnp.concatenate([block, jnp.zeros((XROWS - HALF, 128), F32)], axis=0).astype(BF16)

    @pl.when(x.own)
    def _():
        xall[slot, seq] = block

    x.slot_send()
    stepped_t[...] = jnp.transpose(stepped)
    stepped_copy = pltpu.make_async_copy(stepped_t, stepped_out, local_sem.at[0])
    stepped_copy.start()

    wide = weight.astype(F32)
    centred[...] = wide - jnp.mean(wide, axis=1, keepdims=True)
    own_rows = PATCH + MROWS
    for c in range(CHUNKS):
        lanes = slice(128 * c, 128 * c + 128)
        gain = 1.0 + block_mod[0, 0:1, lanes]
        high, low = split(block_mod[0, 1:2, lanes], 2)
        lhs[0:PATCH, lanes] = (centred[:, lanes] * gain).astype(BF16)
        shifts = jnp.where(sub == 0, high.astype(F32), jnp.where(sub == 1, low.astype(F32), 0.0))
        lhs[PATCH:own_rows, lanes] = shifts.astype(BF16)
    found = jnp.dot(lhs[0:own_rows, :], q_weight[...], preferred_element_type=F32)
    a_q = found[0:PATCH]
    b_q = jnp.sum(found[PATCH:own_rows], axis=0, keepdims=True)

    def build(k):
        sources = [m.source(2 * k + e, mine) for e in range(2) for mine in (True, False)]

        for at, src in enumerate(sources):
            first = at * own_rows

            for p in range(SEQ):
                mods = mall[src, p].astype(F32)
                for r in range(PARTS):
                    lanes = slice(p * FEAT + 128 * r, p * FEAT + 128 * r + 128)
                    lhs[first : first + PATCH, lanes] = (centred[:, lanes] * mods[r : r + 1]).astype(BF16)
                    kept = jnp.where((sub == PARTS + r) | (sub == 2 * PARTS + r), mods, 0.0)
                    lhs[first + PATCH : first + own_rows, lanes] = kept.astype(BF16)

        found = jnp.dot(lhs[...], kv_weight[...], preferred_element_type=F32)
        for at, src in enumerate(sources):
            first = at * own_rows
            a_kv[src] = found[first : first + PATCH].astype(BF16)
            b_kv[src] = jnp.broadcast_to(
                jnp.sum(found[first + PATCH : first + own_rows], axis=0, keepdims=True), (8, 2 * HD)
            )

    def tokens(src, matrix, bias):
        blocks = xall[src].reshape(SEQ * XROWS, 128)
        zero = jnp.zeros_like(matrix)
        found = []
        for pair in ([matrix, zero], [zero, matrix]):
            wide = jnp.dot(blocks, jnp.concatenate(pair, axis=0), preferred_element_type=F32)
            wide = wide.reshape(SEQ, XROWS, wide.shape[1])[:, 0:HALF]
            found.append(wide.reshape(SEQ * HALF, wide.shape[2]) + bias)
        return found

    pairs = ((keys_a, values_a), (keys_b, values_b))
    group = SEQ * HALF
    mine = slot_group[slot]

    def prepare(i, keys, values):
        for at, own in enumerate((True, False)):
            src = x.source(i, own)
            b = lax.rem(src + 1, SLOTS)
            keep = jnp.full((1, HD), group_mask[mine, slot_group[b]], jnp.int32).astype(F32)
            for half, t in enumerate(tokens(src, a_kv[b], b_kv[b][0:1])):
                rows = slice((2 * at + half) * group, (2 * at + half + 1) * group)
                keys[rows, :] = unit(t[:, 0:HD]).astype(BF16)
                values[rows, 0:HD] = (t[:, HD : 2 * HD] * keep).astype(BF16)
                values[rows, HD : 2 * HD] = jnp.broadcast_to(keep, (group, HD)).astype(BF16)

    def attend(i):
        keys, values = pairs[i % 2]
        prepare(i, keys, values)
        scores = lax.dot_general(q_ref[...], keys[...], NT, preferred_element_type=F32)
        probs = jnp.exp2(scores).astype(BF16)
        total[...] += jnp.dot(probs, values[...], preferred_element_type=F32)

    total[...] = jnp.zeros_like(total)
    def queries():
        scale = 1.0 / (math.sqrt(HD) * math.log(2.0))
        for half, t in enumerate(tokens(lax.rem(slot + SLOTS - 1, SLOTS), a_q.astype(BF16), b_q)):
            q_ref[half * group : half * group + group, :] = (unit(t) * scale).astype(BF16)

    def run(what, first, last):
        for i in range(first, last + 1):
            what(i)

    run(m.first, 0, 7)
    run(x.first, 0, 1)
    run(m.second, 0, 3)
    run(x.first, 2, 3)
    run(m.second, 4, 7)
    run(x.first, 4, 5)
    run(m.third, 0, 3)
    run(x.first, 6, 7)
    run(x.second, 0, 1)
    run(m.fourth, 0, 1)
    build(0)
    run(m.third, 4, 7)
    run(x.second, 2, 3)
    run(m.fourth, 2, 3)
    build(1)
    run(x.third, 0, 1)
    run(x.second, 4, 5)
    run(m.fourth, 4, 5)
    build(2)
    run(x.second, 6, 7)
    run(x.third, 2, 3)
    run(m.fourth, 6, 7)
    build(3)
    run(x.fourth, 0, 1)
    queries()
    attend(0)
    run(x.third, 4, 5)
    attend(1)
    run(x.third, 6, 7)
    for i in range(2, PAIRS):
        x.fourth(i)
        attend(i)

    for p in range(SEQ):
        found = []
        for half in range(2):
            rows = slice(half * group + p * HALF, half * group + p * HALF + HALF)
            found.append(total[rows, 0:HD] / total[rows, HD : 2 * HD])
        attn[p * TOK : p * TOK + TOK, :] = jnp.concatenate(found, axis=0).astype(attn.dtype)
    attn_copy = pltpu.make_async_copy(attn, attn_out, local_sem.at[1])
    attn_copy.start()
    for copy in sends:
        copy.wait_send()
    m.finish()
    x.finish()
    stepped_copy.wait()
    attn_copy.wait()


def spread_sems():
    dma = pltpu.SemaphoreType.DMA
    return [dma((SLOTS,)) for _ in range(8)]


def local(
    hidden,
    final_mod,
    head_weight,
    latents,
    fresh_noise,
    step_index,
    slot_group,
    group_mask,
    patch_weight,
    block_mod,
    qkv_weight,
):
    hbm = pl.BlockSpec(memory_space=pl.ANY)
    dma = pltpu.SemaphoreType.DMA
    vmem = pltpu.VMEM
    smem = pltpu.SMEM
    stepped_t, attn = pl.pallas_call(
        kernel,
        out_shape=(
            jax.ShapeDtypeStruct((PATCH, TOK), F32),
            jax.ShapeDtypeStruct((SEQ * TOK, HD), BF16),
        ),
        in_specs=[hbm] * 11,
        out_specs=(hbm, hbm),
        scratch_shapes=[
            vmem((TOK, D // HEADS), BF16),
            vmem((1, 2, D // HEADS), F32),
            vmem((PATCH, D // HEADS), F32),
            vmem((PATCH, TOK), F32),
            vmem((PATCH, TOK), F32),
            smem((SLOTS,), jnp.int32),
            smem((SLOTS,), jnp.int32),
            smem((SLOTS, SLOTS), jnp.int32),
            vmem((PATCH, D), BF16),
            vmem((1, 2, D), F32),
            vmem((D, HD), BF16),
            vmem((D, 2 * HD), BF16),
            vmem((PATCH, TOK), F32),
            vmem((SEQ * TOK, HD), BF16),
            vmem((SLOTS, SEQ, XROWS, 128), BF16),
            vmem((SLOTS, SEQ, MROWS, 128), BF16),
            vmem((XROWS, 128), F32),
            vmem((HEADS - 1, XROWS, 128), F32),
            vmem((PATCH, D), F32),
            vmem((4 * (PATCH + MROWS), D), BF16),
            vmem((SLOTS, PATCH, 2 * HD), BF16),
            vmem((SLOTS, 8, 2 * HD), F32),
            vmem((SEQ * TOK, HD), BF16),
            vmem((KEYS, HD), BF16),
            vmem((KEYS, 2 * HD), BF16),
            vmem((KEYS, HD), BF16),
            vmem((KEYS, 2 * HD), BF16),
            vmem((SEQ * TOK, 2 * HD), F32),
            dma((13,)),
            dma((HEADS - 1,)),
            dma((HEADS - 1,)),
        ]
        + spread_sems()
        + spread_sems(),
        compiler_params=pltpu.CompilerParams(
            collective_id=0, has_side_effects=True, vmem_limit_bytes=56 * 2**20
        ),
        name="window",
    )(
        hidden,
        final_mod,
        head_weight.T,
        latents.T,
        fresh_noise.T,
        step_index,
        slot_group,
        group_mask,
        patch_weight,
        block_mod,
        jnp.transpose(qkv_weight, (1, 0, 2)),
    )
    return stepped_t.T, attn


def solution(mesh):
    in_specs = (
        P(("slot", "seq"), "head"),
        P("slot", None, "head"),
        P("head", None),
        P(("slot", "seq"), None),
        P("seq", None),
        P(),
        P(),
        P(),
        P(),
        P("slot", None, None),
        P(None, None, ("seq", "head")),
    )
    out_specs = (P(("slot", "seq"), None), P("slot", ("seq", "head")))
    return jax.shard_map(local, mesh=mesh, in_specs=in_specs, out_specs=out_specs, check_vma=False)
```

```python
import math

import jax
import jax.numpy as jnp
from jax import lax
from jax.experimental import pallas as pl
from jax.experimental.pallas import tpu as pltpu
from jax.sharding import PartitionSpec as P

D = 5120
HD = 128
STEPS = 48
PATCH = 64
SLOTS = 16
SEQ = 8
HEADS = 4
CHUNKS = D // 128
TOK = 80
HALF = 40
XROWS = 48
MROWS = 16
FEAT = D // SEQ
EPS = 1e-06
MESH = pl.DeviceIdType.MESH
HIGHEST = lax.Precision.HIGHEST
F32 = jnp.float32
BF16 = jnp.bfloat16
NT = (((1,), (1,)), ((), ()))
PAIRS = SLOTS // 2
ROW = SEQ // 2
PARTS = FEAT // 128
KEYS = 2 * SEQ * TOK


def remote(src, dst, send_sem, recv_sem, device_id):
    return pltpu.make_async_remote_copy(
        src_ref=src,
        dst_ref=dst,
        send_sem=send_sem,
        recv_sem=recv_sem,
        device_id=device_id,
        device_id_type=MESH,
    )


class Spread:
    def __init__(self, buf, shift, direct, sems):
        self.buf = buf
        self.direct = direct
        self.zs, self.zr, self.qs, self.qr, self.ys, self.yr, self.cs, self.cr = sems
        self.shift = shift
        self.slot = lax.axis_index("slot")
        self.seq = lax.axis_index("seq")
        self.head = lax.axis_index("head")
        self.core = lax.rem(self.head, 2)
        self.own = lax.rem(self.slot, 2) == self.core
        self.other_core = self.head + 1 - 2 * self.core
        self.low = self.seq // ROW
        self.at = lax.rem(self.seq, ROW)

    def source(self, i, mine=True):
        odd = lax.rem(i, 2) == 1
        even_list = jnp.where(odd, i + 1, SLOTS - i)
        odd_list = jnp.where(odd, i, SLOTS - 1 - i)
        if self.shift:
            even_list, odd_list = odd_list + 1, even_list + 1
        near = jnp.where(self.own, even_list, odd_list) if mine else jnp.where(self.own, odd_list, even_list)
        return lax.rem(self.slot + near, SLOTS)

    def half(self, src, low):
        return self.buf.at[src, pl.ds(low * ROW, ROW)]

    def slot_copy(self, k):
        block = self.buf.at[self.slot, self.seq]
        return remote(
            block, block, self.zs.at[k], self.zr.at[self.slot], {"slot": lax.rem(self.slot + k, SLOTS)}
        )

    def slot_send(self):
        @pl.when(self.own)
        def _():
            for k in range(1, SLOTS):
                self.slot_copy(k // 2 if k % 2 == 0 else SLOTS - (k + 1) // 2).start()

    def slot_wait(self, i):
        src = self.source(i)
        block = self.buf.at[src, self.seq]

        @pl.when(src != self.slot)
        def _():
            remote(block, block, self.zs.at[0], self.zr.at[src], {"slot": self.slot}).wait_recv()

    def row_send(self, i):
        src = self.source(i)
        block = self.buf.at[src, self.seq]
        peers = SEQ if self.direct else ROW
        for k in range(1, peers):
            to = lax.rem(self.seq + k, SEQ) if self.direct else self.low * ROW + lax.rem(self.at + k, ROW)
            remote(block, block, self.qs.at[src], self.qr.at[src], {"seq": to}).start()

    def row_all(self, src):
        blocks = self.buf.at[src, pl.ds(0, (SEQ if self.direct else ROW) - 1)]
        return remote(blocks, blocks, self.qs.at[src], self.qr.at[src], {"seq": self.seq})

    def side_copy(self, i):
        src = self.source(i)
        blocks = self.half(src, self.low)
        head = lax.rem(self.head + 2 * lax.rem(i, 2), HEADS)
        seq = (1 - self.low) * ROW + self.at
        return remote(blocks, blocks, self.ys.at[src], self.yr.at[src], {"seq": seq, "head": head})

    def core_copy(self, src, low):
        blocks = self.half(src, low)
        return remote(blocks, blocks, self.cs.at[src], self.cr.at[src], {"head": self.other_core})

    def core_all(self, src):
        blocks = self.buf.at[src]
        return remote(blocks, blocks, self.cs.at[src], self.cr.at[src], {"head": self.other_core})

    def first(self, i):
        self.slot_wait(i)
        self.row_send(i)

    def second(self, i):
        src = self.source(i)
        self.row_all(src).wait_recv()
        if self.direct:
            self.core_all(src).start()
            return
        self.side_copy(i).start()
        self.core_copy(src, self.low).start()

    def third(self, i):
        src = self.source(i)
        self.side_copy(i).wait_recv()
        self.core_copy(src, 1 - self.low).start()

    def fourth(self, i):
        self.core_all(self.source(i, mine=False)).wait_recv()

    def finish(self):
        @pl.when(self.own)
        def _():
            @pl.loop(1, SLOTS)
            def _(k):
                self.slot_copy(k).wait_send()

        @pl.loop(0, PAIRS)
        def _(i):
            src = self.source(i)
            self.row_all(src).wait_send()
            if not self.direct:
                self.side_copy(i).wait_send()
            self.core_all(src).wait_send()


def split(value, count):
    found = []
    for _ in range(count):
        part = value.astype(BF16)
        found.append(part)
        value = value - part.astype(F32)
    return found


def partial_velocity(hidden, final_mod, head_t, msg):
    h = hidden[...]
    wide = h.astype(F32)
    mean = jnp.mean(wide, axis=1, keepdims=True)
    centred = wide - mean
    spread = jnp.sum(centred * centred, axis=1, keepdims=True)
    gained = head_t[...] * (1.0 + final_mod[0, 0:1, :])
    gain_sum = jnp.sum(gained, axis=1, keepdims=True)
    shift_sum = jnp.sum(head_t[...] * final_mod[0, 1:2, :], axis=1, keepdims=True)
    stack = jnp.concatenate(split(gained, 3), axis=0)
    parts = lax.dot_general(h, stack, NT, preferred_element_type=F32)
    part = parts[:, 0:PATCH] + parts[:, PATCH : 2 * PATCH] + parts[:, 2 * PATCH : 3 * PATCH]
    lane = lax.broadcasted_iota(jnp.int32, (TOK, 128), 1)
    pad = jnp.zeros((TOK - PATCH, 1), F32)
    gain_sum = jnp.concatenate([gain_sum, pad], axis=0)
    shift_sum = jnp.concatenate([shift_sum, pad], axis=0)
    stats = jnp.where(lane == 0, mean, jnp.where(lane == 1, spread, 0.0))
    stats = jnp.where(lane == 2, gain_sum, jnp.where(lane == 3, shift_sum, stats))
    stats = jnp.transpose(jnp.concatenate([stats, jnp.zeros((128 - TOK, 128), F32)], axis=0))
    msg[0:HALF, :] = jnp.concatenate([part[0:HALF], part[HALF:TOK]], axis=1)
    msg[HALF:XROWS, :] = stats[0:8]


def whole_velocity(parts, count):
    total = sum(parts)
    mean = total[HALF : HALF + 1] / len(parts)
    spread = total[HALF + 1 : HALF + 2]
    for p in parts:
        off = p[HALF : HALF + 1] - mean
        spread = spread + count * off * off
    scale = lax.rsqrt(spread / (count * len(parts)) + EPS)
    turned = jnp.transpose(jnp.concatenate([mean, scale, jnp.zeros((126, 128), F32)], axis=0))[0:TOK]
    gain_row = total[HALF + 2 : HALF + 3, 0:PATCH]
    shift_row = total[HALF + 3 : HALF + 4, 0:PATCH]
    product = jnp.concatenate([total[0:HALF, 0:PATCH], total[0:HALF, PATCH:128]], axis=0)
    return (product - turned[:, 0:1] * gain_row) * turned[:, 1:2] + shift_row


def sigma_of(level):
    ratio = jnp.full((1, PATCH), level, jnp.int32).astype(F32) / STEPS
    return 5.0 * ratio / (1.0 + 4.0 * ratio)


def unit(block):
    return block * lax.rsqrt(jnp.mean(block * block, axis=1, keepdims=True) + EPS)


def kernel(
    hidden_in,
    final_mod_in,
    head_in,
    latents_in,
    noise_in,
    step_in,
    group_in,
    mask_in,
    patch_in,
    block_in,
    qkv_in,
    stepped_out,
    attn_out,
    hidden,
    final_mod,
    head_t,
    latents_t,
    noise_t,
    step_index,
    slot_group,
    group_mask,
    patch_weight,
    block_mod,
    q_weight,
    kv_weight,
    stepped_t,
    attn,
    xall,
    mall,
    msg,
    got,
    centred,
    lhs,
    a_kv,
    b_kv,
    q_ref,
    keys_a,
    values_a,
    keys_b,
    values_b,
    total,
    local_sem,
    ps,
    pr,
    *sems,
):
    x = Spread(xall, 0, False, sems[:8])
    m = Spread(mall, 1, True, sems[8:])
    slot, seq, head = x.slot, x.seq, x.head
    loads = [
        pltpu.make_async_copy(src, dst, local_sem.at[i])
        for i, (src, dst) in enumerate(
            (
                (hidden_in, hidden),
                (final_mod_in, final_mod),
                (head_in, head_t),
                (block_in, block_mod),
                (patch_in, patch_weight),
                (latents_in, latents_t),
                (noise_in, noise_t),
                (step_in, step_index),
                (group_in, slot_group),
                (mask_in, group_mask),
                (qkv_in.at[0], q_weight),
                (qkv_in.at[1], kv_weight.at[:, 0:HD]),
                (qkv_in.at[2], kv_weight.at[:, HD : 2 * HD]),
            )
        )
    ]
    for copy in loads:
        copy.start()
    barrier = pltpu.get_barrier_semaphore()

    def greet(device_id):
        pl.semaphore_signal(barrier, inc=1, device_id=device_id, device_id_type=MESH)

    for k in range(1, SLOTS):
        greet({"slot": lax.rem(slot + k, SLOTS)})
    for k in range(1, HEADS):
        greet({"head": lax.rem(head + k, HEADS)})
    for k in range(1, SEQ):
        greet({"seq": lax.rem(seq + k, SEQ)})
    side = (1 - x.low) * ROW + x.at
    greet({"seq": side, "head": lax.rem(head + 2, HEADS)})

    for copy in loads[:4]:
        copy.wait()
    partial_velocity(hidden, final_mod, head_t, msg)
    sub = lax.broadcasted_iota(jnp.int32, (MROWS, 128), 0)

    @pl.when(x.own)
    def _():
        start = pl.multiple_of(seq * FEAT, 128)
        gain = 1.0 + block_mod[0, 0:1, pl.ds(start, FEAT)]
        high, low = split(block_mod[0, 1:2, pl.ds(start, FEAT)], 2)
        rows = []
        for row in (gain, high.astype(F32), low.astype(F32)):
            rows += [row[:, 128 * r : 128 * r + 128] for r in range(PARTS)]
        rows += [jnp.zeros((1, 128), F32)]
        mall[slot, seq] = jnp.concatenate(rows, axis=0).astype(BF16)

    pl.semaphore_wait(barrier, SLOTS + HEADS + SEQ - 3 + 1)
    sends = [
        remote(msg, got.at[k - 1], ps.at[k - 1], pr.at[k - 1], {"head": lax.rem(head + k, HEADS)})
        for k in range(1, HEADS)
    ]
    for copy in sends:
        copy.start()
    m.slot_send()

    for copy in loads[4:]:
        copy.wait()
    weight = patch_weight[...]
    gram = lax.dot_general(weight, weight, NT, preferred_element_type=F32) / D
    ones = jnp.ones((16, D), BF16)
    mean_row = lax.dot_general(ones, weight, NT, preferred_element_type=F32)[0:8] / D
    mean_outer = lax.dot_general(
        mean_row, mean_row, (((0,), (0,)), ((), ())), precision=HIGHEST, preferred_element_type=F32
    ) / 8.0
    gram = gram - mean_outer
    latents = jnp.transpose(latents_t[...])
    noise = jnp.transpose(noise_t[...])
    now = step_index[slot]
    later = jnp.where(slot == SLOTS - 1, 0, step_index[jnp.minimum(slot + 1, SLOTS - 1)])
    delta = sigma_of(later) - sigma_of(now)

    for copy in sends:
        copy.wait_recv()
    velocity = whole_velocity([msg[...]] + [got[k] for k in range(HEADS - 1)], D // HEADS)
    stepped = latents + delta * velocity
    shifted = jnp.where(slot == SLOTS - 1, noise, stepped).astype(BF16).astype(F32)
    projected = jnp.dot(shifted, gram, precision=HIGHEST, preferred_element_type=F32)
    spread = jnp.sum(projected * shifted, axis=1, keepdims=True)
    scaled = shifted * lax.rsqrt(jnp.maximum(spread, 0.0) + EPS)
    block = jnp.concatenate([scaled[0:HALF], scaled[HALF:TOK]], axis=1)
    block = jnp.concatenate([block, jnp.zeros((XROWS - HALF, 128), F32)], axis=0).astype(BF16)

    @pl.when(x.own)
    def _():
        xall[slot, seq] = block

    x.slot_send()
    stepped_t[...] = jnp.transpose(stepped)
    stepped_copy = pltpu.make_async_copy(stepped_t, stepped_out, local_sem.at[0])
    stepped_copy.start()

    wide = weight.astype(F32)
    centred[...] = wide - jnp.mean(wide, axis=1, keepdims=True)
    own_rows = PATCH + MROWS
    for c in range(CHUNKS):
        lanes = slice(128 * c, 128 * c + 128)
        gain = 1.0 + block_mod[0, 0:1, lanes]
        high, low = split(block_mod[0, 1:2, lanes], 2)
        lhs[0:PATCH, lanes] = (centred[:, lanes] * gain).astype(BF16)
        shifts = jnp.where(sub == 0, high.astype(F32), jnp.where(sub == 1, low.astype(F32), 0.0))
        lhs[PATCH:own_rows, lanes] = shifts.astype(BF16)
    found = jnp.dot(lhs[0:own_rows, :], q_weight[...], preferred_element_type=F32)
    a_q = found[0:PATCH]
    b_q = jnp.sum(found[PATCH:own_rows], axis=0, keepdims=True)

    def build(k):
        sources = [m.source(2 * k + e, mine) for e in range(2) for mine in (True, False)]

        for at, src in enumerate(sources):
            first = at * own_rows

            for p in range(SEQ):
                mods = mall[src, p].astype(F32)
                for r in range(PARTS):
                    lanes = slice(p * FEAT + 128 * r, p * FEAT + 128 * r + 128)
                    lhs[first : first + PATCH, lanes] = (centred[:, lanes] * mods[r : r + 1]).astype(BF16)
                    kept = jnp.where((sub == PARTS + r) | (sub == 2 * PARTS + r), mods, 0.0)
                    lhs[first + PATCH : first + own_rows, lanes] = kept.astype(BF16)

        found = jnp.dot(lhs[...], kv_weight[...], preferred_element_type=F32)
        for at, src in enumerate(sources):
            first = at * own_rows
            a_kv[src] = found[first : first + PATCH].astype(BF16)
            b_kv[src] = jnp.broadcast_to(
                jnp.sum(found[first + PATCH : first + own_rows], axis=0, keepdims=True), (8, 2 * HD)
            )

    def tokens(src, matrix, bias):
        blocks = xall[src].reshape(SEQ * XROWS, 128)
        zero = jnp.zeros_like(matrix)
        found = []
        for pair in ([matrix, zero], [zero, matrix]):
            wide = jnp.dot(blocks, jnp.concatenate(pair, axis=0), preferred_element_type=F32)
            wide = wide.reshape(SEQ, XROWS, wide.shape[1])[:, 0:HALF]
            found.append(wide.reshape(SEQ * HALF, wide.shape[2]) + bias)
        return found

    pairs = ((keys_a, values_a), (keys_b, values_b))
    group = SEQ * HALF
    mine = slot_group[slot]

    def prepare(i, own):
        keys, values = pairs[i % 2]
        src = x.source(i, own)
        b = lax.rem(src + 1, SLOTS)
        keep = jnp.full((1, HD), group_mask[mine, slot_group[b]], jnp.int32).astype(F32)
        for half, t in enumerate(tokens(src, a_kv[b], b_kv[b][0:1])):
            first = (half if own else 2 + half) * group
            rows = slice(first, first + group)
            keys[rows, :] = unit(t[:, 0:HD]).astype(BF16)
            values[rows, 0:HD] = (t[:, HD : 2 * HD] * keep).astype(BF16)
            values[rows, HD : 2 * HD] = jnp.broadcast_to(keep, (group, HD)).astype(BF16)

    def attend(i):
        keys, values = pairs[i % 2]
        scores = lax.dot_general(q_ref[...], keys[...], NT, preferred_element_type=F32)
        probs = jnp.exp2(scores).astype(BF16)
        total[...] += jnp.dot(probs, values[...], preferred_element_type=F32)

    total[...] = jnp.zeros_like(total)
    def queries():
        scale = 1.0 / (math.sqrt(HD) * math.log(2.0))
        for half, t in enumerate(tokens(lax.rem(slot + SLOTS - 1, SLOTS), a_q.astype(BF16), b_q)):
            q_ref[half * group : half * group + group, :] = (unit(t) * scale).astype(BF16)

    def run(what, first, last):
        for i in range(first, last + 1):
            what(i)

    run(m.first, 0, 7)
    run(x.first, 0, 1)
    run(m.second, 0, 1)
    run(x.first, 2, 3)
    run(m.second, 2, 3)
    run(m.fourth, 0, 1)
    build(0)
    run(x.first, 4, 5)
    run(m.second, 4, 5)
    run(m.fourth, 2, 3)
    build(1)
    run(x.first, 6, 6)
    run(x.second, 0, 0)
    run(m.second, 6, 7)
    run(m.fourth, 4, 5)
    run(x.first, 7, 7)
    build(2)
    run(x.second, 1, 2)
    run(m.fourth, 6, 7)
    build(3)
    run(x.third, 0, 0)
    run(x.second, 3, 3)
    run(x.fourth, 0, 0)
    queries()
    for i in range(PAIRS):
        if i + 4 < PAIRS:
            x.second(i + 4)
        if i + 1 < PAIRS:
            x.third(i + 1)
        prepare(i, True)
        if i > 0:
            x.fourth(i)
        prepare(i, False)
        attend(i)

    for p in range(SEQ):
        found = []
        for half in range(2):
            rows = slice(half * group + p * HALF, half * group + p * HALF + HALF)
            found.append(total[rows, 0:HD] / total[rows, HD : 2 * HD])
        attn[p * TOK : p * TOK + TOK, :] = jnp.concatenate(found, axis=0).astype(attn.dtype)
    attn_copy = pltpu.make_async_copy(attn, attn_out, local_sem.at[1])
    attn_copy.start()
    for copy in sends:
        copy.wait_send()
    m.finish()
    x.finish()
    stepped_copy.wait()
    attn_copy.wait()


def spread_sems():
    dma = pltpu.SemaphoreType.DMA
    return [dma((SLOTS,)) for _ in range(8)]


def local(
    hidden,
    final_mod,
    head_weight,
    latents,
    fresh_noise,
    step_index,
    slot_group,
    group_mask,
    patch_weight,
    block_mod,
    qkv_weight,
):
    hbm = pl.BlockSpec(memory_space=pl.ANY)
    dma = pltpu.SemaphoreType.DMA
    vmem = pltpu.VMEM
    smem = pltpu.SMEM
    stepped_t, attn = pl.pallas_call(
        kernel,
        out_shape=(
            jax.ShapeDtypeStruct((PATCH, TOK), F32),
            jax.ShapeDtypeStruct((SEQ * TOK, HD), BF16),
        ),
        in_specs=[hbm] * 11,
        out_specs=(hbm, hbm),
        scratch_shapes=[
            vmem((TOK, D // HEADS), BF16),
            vmem((1, 2, D // HEADS), F32),
            vmem((PATCH, D // HEADS), F32),
            vmem((PATCH, TOK), F32),
            vmem((PATCH, TOK), F32),
            smem((SLOTS,), jnp.int32),
            smem((SLOTS,), jnp.int32),
            smem((SLOTS, SLOTS), jnp.int32),
            vmem((PATCH, D), BF16),
            vmem((1, 2, D), F32),
            vmem((D, HD), BF16),
            vmem((D, 2 * HD), BF16),
            vmem((PATCH, TOK), F32),
            vmem((SEQ * TOK, HD), BF16),
            vmem((SLOTS, SEQ, XROWS, 128), BF16),
            vmem((SLOTS, SEQ, MROWS, 128), BF16),
            vmem((XROWS, 128), F32),
            vmem((HEADS - 1, XROWS, 128), F32),
            vmem((PATCH, D), F32),
            vmem((4 * (PATCH + MROWS), D), BF16),
            vmem((SLOTS, PATCH, 2 * HD), BF16),
            vmem((SLOTS, 8, 2 * HD), F32),
            vmem((SEQ * TOK, HD), BF16),
            vmem((KEYS, HD), BF16),
            vmem((KEYS, 2 * HD), BF16),
            vmem((KEYS, HD), BF16),
            vmem((KEYS, 2 * HD), BF16),
            vmem((SEQ * TOK, 2 * HD), F32),
            dma((13,)),
            dma((HEADS - 1,)),
            dma((HEADS - 1,)),
        ]
        + spread_sems()
        + spread_sems(),
        compiler_params=pltpu.CompilerParams(
            collective_id=0, has_side_effects=True, vmem_limit_bytes=56 * 2**20
        ),
        name="window",
    )(
        hidden,
        final_mod,
        head_weight.T,
        latents.T,
        fresh_noise.T,
        step_index,
        slot_group,
        group_mask,
        patch_weight,
        block_mod,
        jnp.transpose(qkv_weight, (1, 0, 2)),
    )
    return stepped_t.T, attn


def solution(mesh):
    in_specs = (
        P(("slot", "seq"), "head"),
        P("slot", None, "head"),
        P("head", None),
        P(("slot", "seq"), None),
        P("seq", None),
        P(),
        P(),
        P(),
        P(),
        P("slot", None, None),
        P(None, None, ("seq", "head")),
    )
    out_specs = (P(("slot", "seq"), None), P("slot", ("seq", "head")))
    return jax.shard_map(local, mesh=mesh, in_specs=in_specs, out_specs=out_specs, check_vma=False)
```

```python
import math

import jax
import jax.numpy as jnp
from jax import lax
from jax.experimental import pallas as pl
from jax.experimental.pallas import tpu as pltpu
from jax.sharding import PartitionSpec as P

D = 5120
HD = 128
STEPS = 48
PATCH = 64
SLOTS = 16
SEQ = 8
HEADS = 4
CHUNKS = D // 128
TOK = 80
HALF = 40
XROWS = 48
MROWS = 16
FEAT = D // SEQ
EPS = 1e-06
MESH = pl.DeviceIdType.MESH
HIGHEST = lax.Precision.HIGHEST
F32 = jnp.float32
BF16 = jnp.bfloat16
NT = (((1,), (1,)), ((), ()))
PAIRS = SLOTS // 2
ROW = SEQ // 2
RELAYED = 8
ORDER = (
    ("mf", 0), ("mf", 1), ("mf", 2), ("mf", 3), ("mf", 4), ("mf", 5), ("xf", 0), ("xf", 1), ("ms", 0),
    ("ms", 1), ("mf", 6), ("mf", 7), ("xf", 2), ("xf", 3), ("ms", 2), ("ms", 3), ("mh", 0), ("mh", 1),
    ("B", 0), ("xf", 4), ("xf", 5), ("ms", 4), ("ms", 5), ("mh", 2), ("mh", 3), ("xs", 0), ("xs", 1),
    ("B", 1), ("xf", 6), ("xf", 7), ("xs", 2), ("xs", 3), ("ms", 6), ("ms", 7), ("mh", 4), ("mh", 5),
    ("B", 2), ("xs", 4), ("mh", 6), ("mh", 7), ("xt", 0), ("xt", 1), ("B", 3), ("xs", 5), ("xh", 0),
    ("Q", 0), ("P", 0), ("xs", 6), ("xs", 7), ("xt", 2), ("xt", 3), ("xh", 1), ("P", 1), ("A", 0),
    ("xt", 4), ("xt", 5), ("xh", 2), ("P", 2), ("A", 1), ("xt", 6), ("xt", 7), ("xh", 3), ("P", 3),
    ("A", 2), ("xh", 4), ("P", 4), ("A", 3), ("xh", 5), ("P", 5), ("A", 4), ("xh", 6), ("P", 6),
    ("A", 5), ("xh", 7), ("P", 7), ("A", 6), ("A", 7),
)
PARTS = FEAT // 128
KEYS = 2 * SEQ * TOK


def remote(src, dst, send_sem, recv_sem, device_id):
    return pltpu.make_async_remote_copy(
        src_ref=src,
        dst_ref=dst,
        send_sem=send_sem,
        recv_sem=recv_sem,
        device_id=device_id,
        device_id_type=MESH,
    )


class Spread:
    def __init__(self, buf, shift, relayed, sems):
        self.buf = buf
        self.relayed = relayed
        self.zs, self.zr, self.qs, self.qr, self.ys, self.yr, self.cs, self.cr = sems
        self.shift = shift
        self.slot = lax.axis_index("slot")
        self.seq = lax.axis_index("seq")
        self.head = lax.axis_index("head")
        self.core = lax.rem(self.head, 2)
        self.own = lax.rem(self.slot, 2) == self.core
        self.other_core = self.head + 1 - 2 * self.core
        self.low = self.seq // ROW
        self.at = lax.rem(self.seq, ROW)

    def source(self, i, mine=True):
        odd = lax.rem(i, 2) == 1
        even_list = jnp.where(odd, i + 1, SLOTS - i)
        odd_list = jnp.where(odd, i, SLOTS - 1 - i)
        if self.shift:
            even_list, odd_list = odd_list + 1, even_list + 1
        near = jnp.where(self.own, even_list, odd_list) if mine else jnp.where(self.own, odd_list, even_list)
        return lax.rem(self.slot + near, SLOTS)

    def half(self, src, low):
        return self.buf.at[src, pl.ds(low * ROW, ROW)]

    def slot_copy(self, k):
        block = self.buf.at[self.slot, self.seq]
        return remote(
            block, block, self.zs.at[k], self.zr.at[self.slot], {"slot": lax.rem(self.slot + k, SLOTS)}
        )

    def slot_send(self):
        @pl.when(self.own)
        def _():
            for k in range(1, SLOTS):
                self.slot_copy(k // 2 if k % 2 == 0 else SLOTS - (k + 1) // 2).start()

    def slot_wait(self, i):
        src = self.source(i)
        block = self.buf.at[src, self.seq]

        @pl.when(src != self.slot)
        def _():
            remote(block, block, self.zs.at[0], self.zr.at[src], {"slot": self.slot}).wait_recv()

    def row_send(self, i):
        src = self.source(i)
        block = self.buf.at[src, self.seq]
        relay = i < self.relayed
        for k in range(1, ROW if relay else SEQ):
            to = self.low * ROW + lax.rem(self.at + k, ROW) if relay else lax.rem(self.seq + k, SEQ)
            remote(block, block, self.qs.at[src], self.qr.at[src], {"seq": to}).start()

    def row_all(self, i):
        src = self.source(i)
        blocks = self.buf.at[src, pl.ds(0, (ROW if i < self.relayed else SEQ) - 1)]
        return remote(blocks, blocks, self.qs.at[src], self.qr.at[src], {"seq": self.seq})

    def side_copy(self, i):
        src = self.source(i)
        blocks = self.half(src, self.low)
        head = lax.rem(self.head + 2 * lax.rem(i, 2), HEADS)
        seq = (1 - self.low) * ROW + self.at
        return remote(blocks, blocks, self.ys.at[src], self.yr.at[src], {"seq": seq, "head": head})

    def core_copy(self, src, low):
        blocks = self.half(src, low)
        return remote(blocks, blocks, self.cs.at[src], self.cr.at[src], {"head": self.other_core})

    def core_all(self, src):
        blocks = self.buf.at[src]
        return remote(blocks, blocks, self.cs.at[src], self.cr.at[src], {"head": self.other_core})

    def first(self, i):
        self.slot_wait(i)
        self.row_send(i)

    def second(self, i):
        src = self.source(i)
        self.row_all(i).wait_recv()
        if i >= self.relayed:
            self.core_all(src).start()
            return
        self.side_copy(i).start()
        self.core_copy(src, self.low).start()

    def third(self, i):
        if i >= self.relayed:
            return
        src = self.source(i)
        self.side_copy(i).wait_recv()
        self.core_copy(src, 1 - self.low).start()

    def fourth(self, i):
        self.core_all(self.source(i, mine=False)).wait_recv()

    def finish(self):
        @pl.when(self.own)
        def _():
            @pl.loop(1, SLOTS)
            def _(k):
                self.slot_copy(k).wait_send()

        for i in range(PAIRS):
            self.row_all(i).wait_send()
            if i < self.relayed:
                self.side_copy(i).wait_send()
            self.core_all(self.source(i)).wait_send()


def split(value, count):
    found = []
    for _ in range(count):
        part = value.astype(BF16)
        found.append(part)
        value = value - part.astype(F32)
    return found


def partial_velocity(hidden, final_mod, head_t, msg):
    h = hidden[...]
    wide = h.astype(F32)
    mean = jnp.mean(wide, axis=1, keepdims=True)
    centred = wide - mean
    spread = jnp.sum(centred * centred, axis=1, keepdims=True)
    gained = head_t[...] * (1.0 + final_mod[0, 0:1, :])
    gain_sum = jnp.sum(gained, axis=1, keepdims=True)
    shift_sum = jnp.sum(head_t[...] * final_mod[0, 1:2, :], axis=1, keepdims=True)
    stack = jnp.concatenate(split(gained, 3), axis=0)
    parts = lax.dot_general(h, stack, NT, preferred_element_type=F32)
    part = parts[:, 0:PATCH] + parts[:, PATCH : 2 * PATCH] + parts[:, 2 * PATCH : 3 * PATCH]
    lane = lax.broadcasted_iota(jnp.int32, (TOK, 128), 1)
    pad = jnp.zeros((TOK - PATCH, 1), F32)
    gain_sum = jnp.concatenate([gain_sum, pad], axis=0)
    shift_sum = jnp.concatenate([shift_sum, pad], axis=0)
    stats = jnp.where(lane == 0, mean, jnp.where(lane == 1, spread, 0.0))
    stats = jnp.where(lane == 2, gain_sum, jnp.where(lane == 3, shift_sum, stats))
    stats = jnp.transpose(jnp.concatenate([stats, jnp.zeros((128 - TOK, 128), F32)], axis=0))
    msg[0:HALF, :] = jnp.concatenate([part[0:HALF], part[HALF:TOK]], axis=1)
    msg[HALF:XROWS, :] = stats[0:8]


def whole_velocity(parts, count):
    total = sum(parts)
    mean = total[HALF : HALF + 1] / len(parts)
    spread = total[HALF + 1 : HALF + 2]
    for p in parts:
        off = p[HALF : HALF + 1] - mean
        spread = spread + count * off * off
    scale = lax.rsqrt(spread / (count * len(parts)) + EPS)
    turned = jnp.transpose(jnp.concatenate([mean, scale, jnp.zeros((126, 128), F32)], axis=0))[0:TOK]
    gain_row = total[HALF + 2 : HALF + 3, 0:PATCH]
    shift_row = total[HALF + 3 : HALF + 4, 0:PATCH]
    product = jnp.concatenate([total[0:HALF, 0:PATCH], total[0:HALF, PATCH:128]], axis=0)
    return (product - turned[:, 0:1] * gain_row) * turned[:, 1:2] + shift_row


def sigma_of(level):
    ratio = jnp.full((1, PATCH), level, jnp.int32).astype(F32) / STEPS
    return 5.0 * ratio / (1.0 + 4.0 * ratio)


def unit(block):
    return block * lax.rsqrt(jnp.mean(block * block, axis=1, keepdims=True) + EPS)


def kernel(
    hidden_in,
    final_mod_in,
    head_in,
    latents_in,
    noise_in,
    step_in,
    group_in,
    mask_in,
    patch_in,
    block_in,
    qkv_in,
    stepped_out,
    attn_out,
    hidden,
    final_mod,
    head_t,
    latents_t,
    noise_t,
    step_index,
    slot_group,
    group_mask,
    patch_weight,
    block_mod,
    q_weight,
    kv_weight,
    stepped_t,
    attn,
    xall,
    mall,
    msg,
    got,
    centred,
    lhs,
    a_kv,
    b_kv,
    q_ref,
    keys_a,
    values_a,
    keys_b,
    values_b,
    total,
    local_sem,
    ps,
    pr,
    *sems,
):
    x = Spread(xall, 0, RELAYED, sems[:8])
    m = Spread(mall, 1, 0, sems[8:])
    slot, seq, head = x.slot, x.seq, x.head
    loads = [
        pltpu.make_async_copy(src, dst, local_sem.at[i])
        for i, (src, dst) in enumerate(
            (
                (hidden_in, hidden),
                (final_mod_in, final_mod),
                (head_in, head_t),
                (block_in, block_mod),
                (patch_in, patch_weight),
                (latents_in, latents_t),
                (noise_in, noise_t),
                (step_in, step_index),
                (group_in, slot_group),
                (mask_in, group_mask),
                (qkv_in.at[0], q_weight),
                (qkv_in.at[1], kv_weight.at[:, 0:HD]),
                (qkv_in.at[2], kv_weight.at[:, HD : 2 * HD]),
            )
        )
    ]
    for copy in loads:
        copy.start()
    barrier = pltpu.get_barrier_semaphore()

    def greet(device_id):
        pl.semaphore_signal(barrier, inc=1, device_id=device_id, device_id_type=MESH)

    for k in range(1, SLOTS):
        greet({"slot": lax.rem(slot + k, SLOTS)})
    for k in range(1, HEADS):
        greet({"head": lax.rem(head + k, HEADS)})
    for k in range(1, SEQ):
        greet({"seq": lax.rem(seq + k, SEQ)})
    side = (1 - x.low) * ROW + x.at
    greet({"seq": side, "head": lax.rem(head + 2, HEADS)})

    for copy in loads[:4]:
        copy.wait()
    partial_velocity(hidden, final_mod, head_t, msg)
    sub = lax.broadcasted_iota(jnp.int32, (MROWS, 128), 0)

    @pl.when(x.own)
    def _():
        start = pl.multiple_of(seq * FEAT, 128)
        gain = 1.0 + block_mod[0, 0:1, pl.ds(start, FEAT)]
        high, low = split(block_mod[0, 1:2, pl.ds(start, FEAT)], 2)
        rows = []
        for row in (gain, high.astype(F32), low.astype(F32)):
            rows += [row[:, 128 * r : 128 * r + 128] for r in range(PARTS)]
        rows += [jnp.zeros((1, 128), F32)]
        mall[slot, seq] = jnp.concatenate(rows, axis=0).astype(BF16)

    pl.semaphore_wait(barrier, SLOTS + HEADS + SEQ - 3 + 1)
    sends = [
        remote(msg, got.at[k - 1], ps.at[k - 1], pr.at[k - 1], {"head": lax.rem(head + k, HEADS)})
        for k in range(1, HEADS)
    ]
    for copy in sends:
        copy.start()
    m.slot_send()

    for copy in loads[4:]:
        copy.wait()
    weight = patch_weight[...]
    gram = lax.dot_general(weight, weight, NT, preferred_element_type=F32) / D
    ones = jnp.ones((16, D), BF16)
    mean_row = lax.dot_general(ones, weight, NT, preferred_element_type=F32)[0:8] / D
    mean_outer = lax.dot_general(
        mean_row, mean_row, (((0,), (0,)), ((), ())), precision=HIGHEST, preferred_element_type=F32
    ) / 8.0
    gram = gram - mean_outer
    latents = jnp.transpose(latents_t[...])
    noise = jnp.transpose(noise_t[...])
    now = step_index[slot]
    later = jnp.where(slot == SLOTS - 1, 0, step_index[jnp.minimum(slot + 1, SLOTS - 1)])
    delta = sigma_of(later) - sigma_of(now)

    for copy in sends:
        copy.wait_recv()
    velocity = whole_velocity([msg[...]] + [got[k] for k in range(HEADS - 1)], D // HEADS)
    stepped = latents + delta * velocity
    shifted = jnp.where(slot == SLOTS - 1, noise, stepped).astype(BF16).astype(F32)
    projected = jnp.dot(shifted, gram, precision=HIGHEST, preferred_element_type=F32)
    spread = jnp.sum(projected * shifted, axis=1, keepdims=True)
    scaled = shifted * lax.rsqrt(jnp.maximum(spread, 0.0) + EPS)
    block = jnp.concatenate([scaled[0:HALF], scaled[HALF:TOK]], axis=1)
    block = jnp.concatenate([block, jnp.zeros((XROWS - HALF, 128), F32)], axis=0).astype(BF16)

    @pl.when(x.own)
    def _():
        xall[slot, seq] = block

    x.slot_send()
    stepped_t[...] = jnp.transpose(stepped)
    stepped_copy = pltpu.make_async_copy(stepped_t, stepped_out, local_sem.at[0])
    stepped_copy.start()

    wide = weight.astype(F32)
    centred[...] = wide - jnp.mean(wide, axis=1, keepdims=True)
    own_rows = PATCH + MROWS
    for c in range(CHUNKS):
        lanes = slice(128 * c, 128 * c + 128)
        gain = 1.0 + block_mod[0, 0:1, lanes]
        high, low = split(block_mod[0, 1:2, lanes], 2)
        lhs[0:PATCH, lanes] = (centred[:, lanes] * gain).astype(BF16)
        shifts = jnp.where(sub == 0, high.astype(F32), jnp.where(sub == 1, low.astype(F32), 0.0))
        lhs[PATCH:own_rows, lanes] = shifts.astype(BF16)
    found = jnp.dot(lhs[0:own_rows, :], q_weight[...], preferred_element_type=F32)
    a_q = found[0:PATCH]
    b_q = jnp.sum(found[PATCH:own_rows], axis=0, keepdims=True)

    def build(k):
        sources = [m.source(2 * k + e, mine) for e in range(2) for mine in (True, False)]

        for at, src in enumerate(sources):
            first = at * own_rows

            for p in range(SEQ):
                mods = mall[src, p].astype(F32)
                for r in range(PARTS):
                    lanes = slice(p * FEAT + 128 * r, p * FEAT + 128 * r + 128)
                    lhs[first : first + PATCH, lanes] = (centred[:, lanes] * mods[r : r + 1]).astype(BF16)
                    kept = jnp.where((sub == PARTS + r) | (sub == 2 * PARTS + r), mods, 0.0)
                    lhs[first + PATCH : first + own_rows, lanes] = kept.astype(BF16)

        found = jnp.dot(lhs[...], kv_weight[...], preferred_element_type=F32)
        for at, src in enumerate(sources):
            first = at * own_rows
            a_kv[src] = found[first : first + PATCH].astype(BF16)
            b_kv[src] = jnp.broadcast_to(
                jnp.sum(found[first + PATCH : first + own_rows], axis=0, keepdims=True), (8, 2 * HD)
            )

    def tokens(src, matrix, bias):
        blocks = xall[src].reshape(SEQ * XROWS, 128)
        zero = jnp.zeros_like(matrix)
        found = []
        for pair in ([matrix, zero], [zero, matrix]):
            wide = jnp.dot(blocks, jnp.concatenate(pair, axis=0), preferred_element_type=F32)
            wide = wide.reshape(SEQ, XROWS, wide.shape[1])[:, 0:HALF]
            found.append(wide.reshape(SEQ * HALF, wide.shape[2]) + bias)
        return found

    pairs = ((keys_a, values_a), (keys_b, values_b))
    group = SEQ * HALF
    mine = slot_group[slot]

    def prepare(i, own):
        keys, values = pairs[i % 2]
        src = x.source(i, own)
        b = lax.rem(src + 1, SLOTS)
        keep = jnp.full((1, HD), group_mask[mine, slot_group[b]], jnp.int32).astype(F32)
        for half, t in enumerate(tokens(src, a_kv[b], b_kv[b][0:1])):
            first = (half if own else 2 + half) * group
            rows = slice(first, first + group)
            keys[rows, :] = unit(t[:, 0:HD]).astype(BF16)
            values[rows, 0:HD] = (t[:, HD : 2 * HD] * keep).astype(BF16)
            values[rows, HD : 2 * HD] = jnp.broadcast_to(keep, (group, HD)).astype(BF16)

    def pair(i):
        prepare(i, True)
        prepare(i, False)

    def attend(i):
        keys, values = pairs[i % 2]
        scores = lax.dot_general(q_ref[...], keys[...], NT, preferred_element_type=F32)
        probs = jnp.exp2(scores).astype(BF16)
        total[...] += jnp.dot(probs, values[...], preferred_element_type=F32)

    total[...] = jnp.zeros_like(total)
    def queries():
        scale = 1.0 / (math.sqrt(HD) * math.log(2.0))
        for half, t in enumerate(tokens(lax.rem(slot + SLOTS - 1, SLOTS), a_q.astype(BF16), b_q)):
            q_ref[half * group : half * group + group, :] = (unit(t) * scale).astype(BF16)

    def run(what, first, last):
        for i in range(first, last + 1):
            what(i)

    steps = {
        "mf": m.first,
        "ms": m.second,
        "mh": m.fourth,
        "xf": x.first,
        "xs": x.second,
        "xt": x.third,
        "xh": x.fourth,
        "B": build,
        "P": pair,
        "A": attend,
    }
    for what, i in ORDER:
        if what == "Q":
            queries()
        else:
            steps[what](i)
    for p in range(SEQ):
        found = []
        for half in range(2):
            rows = slice(half * group + p * HALF, half * group + p * HALF + HALF)
            found.append(total[rows, 0:HD] / total[rows, HD : 2 * HD])
        attn[p * TOK : p * TOK + TOK, :] = jnp.concatenate(found, axis=0).astype(attn.dtype)
    attn_copy = pltpu.make_async_copy(attn, attn_out, local_sem.at[1])
    attn_copy.start()
    for copy in sends:
        copy.wait_send()
    m.finish()
    x.finish()
    stepped_copy.wait()
    attn_copy.wait()


def spread_sems():
    dma = pltpu.SemaphoreType.DMA
    return [dma((SLOTS,)) for _ in range(8)]


def local(
    hidden,
    final_mod,
    head_weight,
    latents,
    fresh_noise,
    step_index,
    slot_group,
    group_mask,
    patch_weight,
    block_mod,
    qkv_weight,
):
    hbm = pl.BlockSpec(memory_space=pl.ANY)
    dma = pltpu.SemaphoreType.DMA
    vmem = pltpu.VMEM
    smem = pltpu.SMEM
    stepped_t, attn = pl.pallas_call(
        kernel,
        out_shape=(
            jax.ShapeDtypeStruct((PATCH, TOK), F32),
            jax.ShapeDtypeStruct((SEQ * TOK, HD), BF16),
        ),
        in_specs=[hbm] * 11,
        out_specs=(hbm, hbm),
        scratch_shapes=[
            vmem((TOK, D // HEADS), BF16),
            vmem((1, 2, D // HEADS), F32),
            vmem((PATCH, D // HEADS), F32),
            vmem((PATCH, TOK), F32),
            vmem((PATCH, TOK), F32),
            smem((SLOTS,), jnp.int32),
            smem((SLOTS,), jnp.int32),
            smem((SLOTS, SLOTS), jnp.int32),
            vmem((PATCH, D), BF16),
            vmem((1, 2, D), F32),
            vmem((D, HD), BF16),
            vmem((D, 2 * HD), BF16),
            vmem((PATCH, TOK), F32),
            vmem((SEQ * TOK, HD), BF16),
            vmem((SLOTS, SEQ, XROWS, 128), BF16),
            vmem((SLOTS, SEQ, MROWS, 128), BF16),
            vmem((XROWS, 128), F32),
            vmem((HEADS - 1, XROWS, 128), F32),
            vmem((PATCH, D), F32),
            vmem((4 * (PATCH + MROWS), D), BF16),
            vmem((SLOTS, PATCH, 2 * HD), BF16),
            vmem((SLOTS, 8, 2 * HD), F32),
            vmem((SEQ * TOK, HD), BF16),
            vmem((KEYS, HD), BF16),
            vmem((KEYS, 2 * HD), BF16),
            vmem((KEYS, HD), BF16),
            vmem((KEYS, 2 * HD), BF16),
            vmem((SEQ * TOK, 2 * HD), F32),
            dma((13,)),
            dma((HEADS - 1,)),
            dma((HEADS - 1,)),
        ]
        + spread_sems()
        + spread_sems(),
        compiler_params=pltpu.CompilerParams(
            collective_id=0, has_side_effects=True, vmem_limit_bytes=56 * 2**20
        ),
        name="window",
    )(
        hidden,
        final_mod,
        head_weight.T,
        latents.T,
        fresh_noise.T,
        step_index,
        slot_group,
        group_mask,
        patch_weight,
        block_mod,
        jnp.transpose(qkv_weight, (1, 0, 2)),
    )
    return stepped_t.T, attn


def solution(mesh):
    in_specs = (
        P(("slot", "seq"), "head"),
        P("slot", None, "head"),
        P("head", None),
        P(("slot", "seq"), None),
        P("seq", None),
        P(),
        P(),
        P(),
        P(),
        P("slot", None, None),
        P(None, None, ("seq", "head")),
    )
    out_specs = (P(("slot", "seq"), None), P("slot", ("seq", "head")))
    return jax.shard_map(local, mesh=mesh, in_specs=in_specs, out_specs=out_specs, check_vma=False)
```

```python
import math

import jax
import jax.numpy as jnp
from jax import lax
from jax.experimental import pallas as pl
from jax.experimental.pallas import tpu as pltpu
from jax.sharding import PartitionSpec as P

D = 5120
HD = 128
STEPS = 48
PATCH = 64
SLOTS = 16
SEQ = 8
HEADS = 4
CHUNKS = D // 128
TOK = 80
HALF = 40
XROWS = 48
MROWS = 16
FEAT = D // SEQ
EPS = 1e-06
MESH = pl.DeviceIdType.MESH
HIGHEST = lax.Precision.HIGHEST
F32 = jnp.float32
BF16 = jnp.bfloat16
NT = (((1,), (1,)), ((), ()))
PAIRS = SLOTS // 2
ROW = SEQ // 2
STEPS_EACH = 2
RELAYED = 4
MOD_RELAYED = 0
ORDER = (
    ("mf", 0), ("mf", 1), ("mf", 2), ("xf", 0), ("ms", 0), ("mf", 3), ("xf", 1), ("ms", 1), ("mh", 0),
    ("B", 0), ("xf", 2), ("ms", 2), ("mh", 1), ("xs", 0), ("B", 1), ("xf", 3), ("xs", 1), ("ms", 3),
    ("mh", 2), ("B", 2), ("xs", 2), ("mh", 3), ("xt", 0), ("B", 3), ("xs", 3), ("xt", 1), ("xh", 0),
    ("Q", 0), ("P", 0), ("P", 1), ("A", 0), ("xt", 2), ("xh", 1), ("P", 2), ("A", 1), ("xt", 3),
    ("P", 3), ("A", 2), ("xh", 2), ("P", 4), ("A", 3), ("P", 5), ("A", 4), ("xh", 3), ("P", 6),
    ("A", 5), ("P", 7), ("A", 6), ("A", 7),
)
PARTS = FEAT // 128
KEYS = 2 * SEQ * TOK


def remote(src, dst, send_sem, recv_sem, device_id):
    return pltpu.make_async_remote_copy(
        src_ref=src,
        dst_ref=dst,
        send_sem=send_sem,
        recv_sem=recv_sem,
        device_id=device_id,
        device_id_type=MESH,
    )


def offset(odd, step):
    if odd:
        return step if step % 2 else SLOTS - 1 - step
    return (step + 1 if step % 2 else SLOTS - step) % SLOTS


class Spread:
    def __init__(self, buf, ahead, relayed, sems):
        self.buf = buf
        self.relayed = relayed
        self.zs, self.zr, self.qs, self.qr, self.ys, self.yr, self.cs, self.cr = sems
        self.slot = lax.axis_index("slot")
        self.seq = lax.axis_index("seq")
        self.head = lax.axis_index("head")
        self.core = lax.rem(self.head, 2)
        self.own = lax.rem(self.slot, 2) == self.core
        self.mine = jnp.where(self.own, 0, 1)
        self.other_core = self.head + 1 - 2 * self.core
        self.low = self.seq // ROW
        self.at = lax.rem(self.seq, ROW)
        self.place = {}
        for odd in (0, 1):
            for step in range(PAIRS):
                far = (offset(1 - odd, step) + 1) % SLOTS if ahead else offset(odd, step)
                self.place[far] = (odd, step)

    def slot_copy(self, k):
        odd, step = self.place[SLOTS - k]
        return remote(
            self.buf.at[0, 0, self.seq],
            self.buf.at[odd, step, self.seq],
            self.zs.at[k],
            self.zr.at[step],
            {"slot": lax.rem(self.slot + k, SLOTS)},
        )

    def slot_send(self):
        @pl.when(self.own)
        def _():
            for k in range(1, SLOTS):
                self.slot_copy(k // 2 if k % 2 == 0 else SLOTS - (k + 1) // 2).start()

    def slot_wait(self, step):
        def wait():
            block = self.buf.at[self.mine, step, self.seq]
            remote(block, block, self.zs.at[0], self.zr.at[step], {"slot": self.slot}).wait_recv()

        if step:
            wait()
        else:
            pl.when(jnp.logical_not(self.own))(wait)

    def blocks(self, g, seqs, mine=True):
        steps = pl.ds(g * STEPS_EACH, STEPS_EACH)
        return self.buf.at[self.mine if mine else 1 - self.mine, steps, seqs]

    def copy(self, blocks, send, recv, g, device_id):
        return remote(blocks, blocks, send.at[g], recv.at[g], device_id)

    def row_copy(self, g, k):
        relay = g < self.relayed
        to = self.low * ROW + lax.rem(self.at + k, ROW) if relay else lax.rem(self.seq + k, SEQ)
        return self.copy(self.blocks(g, self.seq), self.qs, self.qr, g, {"seq": to})

    def row_all(self, g):
        count = (ROW if g < self.relayed else SEQ) - 1
        return self.copy(self.blocks(g, pl.ds(0, count)), self.qs, self.qr, g, {"seq": self.seq})

    def side_copy(self, g):
        head = lax.rem(self.head + 2 * (g % 2), HEADS)
        seq = (1 - self.low) * ROW + self.at
        near = self.blocks(g, pl.ds(self.low * ROW, ROW))
        return self.copy(near, self.ys, self.yr, g, {"seq": seq, "head": head})

    def core_copy(self, g, seqs, mine=True):
        return self.copy(self.blocks(g, seqs, mine), self.cs, self.cr, g, {"head": self.other_core})

    def first(self, g):
        for step in range(g * STEPS_EACH, (g + 1) * STEPS_EACH):
            self.slot_wait(step)
        for k in range(1, ROW if g < self.relayed else SEQ):
            self.row_copy(g, k).start()

    def second(self, g):
        self.row_all(g).wait_recv()
        if g < self.relayed:
            self.side_copy(g).start()
            self.core_copy(g, pl.ds(self.low * ROW, ROW)).start()
        else:
            self.core_copy(g, pl.ds(0, SEQ)).start()

    def third(self, g):
        if g < self.relayed:
            self.side_copy(g).wait_recv()
            self.core_copy(g, pl.ds((1 - self.low) * ROW, ROW)).start()

    def fourth(self, g):
        self.core_copy(g, pl.ds(0, SEQ), False).wait_recv()

    def finish(self):
        @pl.when(self.own)
        def _():
            for k in range(1, SLOTS):
                self.slot_copy(k).wait_send()

        for g in range(PAIRS // STEPS_EACH):
            self.row_all(g).wait_send()
            if g < self.relayed:
                self.side_copy(g).wait_send()
            self.core_copy(g, pl.ds(0, SEQ)).wait_send()


def split(value, count):
    found = []
    for _ in range(count):
        part = value.astype(BF16)
        found.append(part)
        value = value - part.astype(F32)
    return found


def partial_velocity(hidden, final_mod, head_t, msg):
    h = hidden[...]
    wide = h.astype(F32)
    mean = jnp.mean(wide, axis=1, keepdims=True)
    centred = wide - mean
    spread = jnp.sum(centred * centred, axis=1, keepdims=True)
    gained = head_t[...] * (1.0 + final_mod[0, 0:1, :])
    gain_sum = jnp.sum(gained, axis=1, keepdims=True)
    shift_sum = jnp.sum(head_t[...] * final_mod[0, 1:2, :], axis=1, keepdims=True)
    stack = jnp.concatenate(split(gained, 3), axis=0)
    parts = lax.dot_general(h, stack, NT, preferred_element_type=F32)
    part = parts[:, 0:PATCH] + parts[:, PATCH : 2 * PATCH] + parts[:, 2 * PATCH : 3 * PATCH]
    lane = lax.broadcasted_iota(jnp.int32, (TOK, 128), 1)
    pad = jnp.zeros((TOK - PATCH, 1), F32)
    gain_sum = jnp.concatenate([gain_sum, pad], axis=0)
    shift_sum = jnp.concatenate([shift_sum, pad], axis=0)
    stats = jnp.where(lane == 0, mean, jnp.where(lane == 1, spread, 0.0))
    stats = jnp.where(lane == 2, gain_sum, jnp.where(lane == 3, shift_sum, stats))
    stats = jnp.transpose(jnp.concatenate([stats, jnp.zeros((128 - TOK, 128), F32)], axis=0))
    msg[0:HALF, :] = jnp.concatenate([part[0:HALF], part[HALF:TOK]], axis=1)
    msg[HALF:XROWS, :] = stats[0:8]


def whole_velocity(parts, count):
    total = sum(parts)
    mean = total[HALF : HALF + 1] / len(parts)
    spread = total[HALF + 1 : HALF + 2]
    for p in parts:
        off = p[HALF : HALF + 1] - mean
        spread = spread + count * off * off
    scale = lax.rsqrt(spread / (count * len(parts)) + EPS)
    turned = jnp.transpose(jnp.concatenate([mean, scale, jnp.zeros((126, 128), F32)], axis=0))[0:TOK]
    gain_row = total[HALF + 2 : HALF + 3, 0:PATCH]
    shift_row = total[HALF + 3 : HALF + 4, 0:PATCH]
    product = jnp.concatenate([total[0:HALF, 0:PATCH], total[0:HALF, PATCH:128]], axis=0)
    return (product - turned[:, 0:1] * gain_row) * turned[:, 1:2] + shift_row


def sigma_of(level):
    ratio = jnp.full((1, PATCH), level, jnp.int32).astype(F32) / STEPS
    return 5.0 * ratio / (1.0 + 4.0 * ratio)


def unit(block):
    return block * lax.rsqrt(jnp.mean(block * block, axis=1, keepdims=True) + EPS)


def kernel(
    hidden_in,
    final_mod_in,
    head_in,
    latents_in,
    noise_in,
    step_in,
    group_in,
    mask_in,
    patch_in,
    block_in,
    qkv_in,
    stepped_out,
    attn_out,
    hidden,
    final_mod,
    head_t,
    latents_t,
    noise_t,
    step_index,
    slot_group,
    group_mask,
    patch_weight,
    block_mod,
    q_weight,
    kv_weight,
    stepped_t,
    attn,
    xall,
    mall,
    msg,
    got,
    centred,
    lhs,
    a_kv,
    b_kv,
    q_ref,
    keys_a,
    values_a,
    keys_b,
    values_b,
    total,
    local_sem,
    ps,
    pr,
    *sems,
):
    x = Spread(xall, False, RELAYED, sems[:8])
    m = Spread(mall, True, MOD_RELAYED, sems[8:])
    slot, seq, head = x.slot, x.seq, x.head
    loads = [
        pltpu.make_async_copy(src, dst, local_sem.at[i])
        for i, (src, dst) in enumerate(
            (
                (hidden_in, hidden),
                (final_mod_in, final_mod),
                (head_in, head_t),
                (block_in, block_mod),
                (patch_in, patch_weight),
                (latents_in, latents_t),
                (noise_in, noise_t),
                (step_in, step_index),
                (group_in, slot_group),
                (mask_in, group_mask),
                (qkv_in.at[0], q_weight),
                (qkv_in.at[1], kv_weight.at[:, 0:HD]),
                (qkv_in.at[2], kv_weight.at[:, HD : 2 * HD]),
            )
        )
    ]
    for copy in loads:
        copy.start()
    barrier = pltpu.get_barrier_semaphore()

    def greet(device_id):
        pl.semaphore_signal(barrier, inc=1, device_id=device_id, device_id_type=MESH)

    for k in range(1, SLOTS):
        greet({"slot": lax.rem(slot + k, SLOTS)})
    for k in range(1, HEADS):
        greet({"head": lax.rem(head + k, HEADS)})
    for k in range(1, SEQ):
        greet({"seq": lax.rem(seq + k, SEQ)})
    side = (1 - x.low) * ROW + x.at
    greet({"seq": side, "head": lax.rem(head + 2, HEADS)})

    for copy in loads[:4]:
        copy.wait()
    partial_velocity(hidden, final_mod, head_t, msg)
    sub = lax.broadcasted_iota(jnp.int32, (MROWS, 128), 0)

    @pl.when(x.own)
    def _():
        start = pl.multiple_of(seq * FEAT, 128)
        gain = 1.0 + block_mod[0, 0:1, pl.ds(start, FEAT)]
        high, low = split(block_mod[0, 1:2, pl.ds(start, FEAT)], 2)
        rows = []
        for row in (gain, high.astype(F32), low.astype(F32)):
            rows += [row[:, 128 * r : 128 * r + 128] for r in range(PARTS)]
        rows += [jnp.zeros((1, 128), F32)]
        mall[0, 0, seq] = jnp.concatenate(rows, axis=0).astype(BF16)

    pl.semaphore_wait(barrier, SLOTS + HEADS + SEQ - 3 + 1)
    sends = [
        remote(msg, got.at[k - 1], ps.at[k - 1], pr.at[k - 1], {"head": lax.rem(head + k, HEADS)})
        for k in range(1, HEADS)
    ]
    for copy in sends:
        copy.start()
    m.slot_send()

    for copy in loads[4:]:
        copy.wait()
    weight = patch_weight[...]
    gram = lax.dot_general(weight, weight, NT, preferred_element_type=F32) / D
    ones = jnp.ones((16, D), BF16)
    mean_row = lax.dot_general(ones, weight, NT, preferred_element_type=F32)[0:8] / D
    mean_outer = lax.dot_general(
        mean_row, mean_row, (((0,), (0,)), ((), ())), precision=HIGHEST, preferred_element_type=F32
    ) / 8.0
    gram = gram - mean_outer
    latents = jnp.transpose(latents_t[...])
    noise = jnp.transpose(noise_t[...])
    now = step_index[slot]
    later = jnp.where(slot == SLOTS - 1, 0, step_index[jnp.minimum(slot + 1, SLOTS - 1)])
    delta = sigma_of(later) - sigma_of(now)

    for copy in sends:
        copy.wait_recv()
    velocity = whole_velocity([msg[...]] + [got[k] for k in range(HEADS - 1)], D // HEADS)
    stepped = latents + delta * velocity
    shifted = jnp.where(slot == SLOTS - 1, noise, stepped).astype(BF16).astype(F32)
    projected = jnp.dot(shifted, gram, precision=HIGHEST, preferred_element_type=F32)
    spread = jnp.sum(projected * shifted, axis=1, keepdims=True)
    scaled = shifted * lax.rsqrt(jnp.maximum(spread, 0.0) + EPS)
    block = jnp.concatenate([scaled[0:HALF], scaled[HALF:TOK]], axis=1)
    block = jnp.concatenate([block, jnp.zeros((XROWS - HALF, 128), F32)], axis=0).astype(BF16)

    @pl.when(x.own)
    def _():
        xall[0, 0, seq] = block

    x.slot_send()
    stepped_t[...] = jnp.transpose(stepped)
    stepped_copy = pltpu.make_async_copy(stepped_t, stepped_out, local_sem.at[0])
    stepped_copy.start()

    wide = weight.astype(F32)
    centred[...] = wide - jnp.mean(wide, axis=1, keepdims=True)
    own_rows = PATCH + MROWS
    for c in range(CHUNKS):
        lanes = slice(128 * c, 128 * c + 128)
        gain = 1.0 + block_mod[0, 0:1, lanes]
        high, low = split(block_mod[0, 1:2, lanes], 2)
        lhs[0:PATCH, lanes] = (centred[:, lanes] * gain).astype(BF16)
        shifts = jnp.where(sub == 0, high.astype(F32), jnp.where(sub == 1, low.astype(F32), 0.0))
        lhs[PATCH:own_rows, lanes] = shifts.astype(BF16)
    found = jnp.dot(lhs[0:own_rows, :], q_weight[...], preferred_element_type=F32)
    a_q = found[0:PATCH]
    b_q = jnp.sum(found[PATCH:own_rows], axis=0, keepdims=True)

    def build(k):
        steps = [(odd, 2 * k + e) for e in range(2) for odd in (0, 1)]
        for at, (odd, step) in enumerate(steps):
            first = at * own_rows
            for p in range(SEQ):
                mods = mall[1 - odd, step, p].astype(F32)
                for r in range(PARTS):
                    lanes = slice(p * FEAT + 128 * r, p * FEAT + 128 * r + 128)
                    lhs[first : first + PATCH, lanes] = (centred[:, lanes] * mods[r : r + 1]).astype(BF16)
                    kept = jnp.where((sub == PARTS + r) | (sub == 2 * PARTS + r), mods, 0.0)
                    lhs[first + PATCH : first + own_rows, lanes] = kept.astype(BF16)

        found = jnp.dot(lhs[...], kv_weight[...], preferred_element_type=F32)
        for at, (odd, step) in enumerate(steps):
            first = at * own_rows
            bias = jnp.sum(found[first + PATCH : first + own_rows], axis=0, keepdims=True)
            a_kv[odd, step] = found[first : first + PATCH].astype(BF16)
            b_kv[odd, step] = jnp.broadcast_to(bias, (8, 2 * HD))

    def tokens(odd, step, matrix, bias):
        blocks = xall[odd, step].reshape(SEQ * XROWS, 128)
        zero = jnp.zeros_like(matrix)
        found = []
        for pair in ([matrix, zero], [zero, matrix]):
            wide = jnp.dot(blocks, jnp.concatenate(pair, axis=0), preferred_element_type=F32)
            wide = wide.reshape(SEQ, XROWS, wide.shape[1])[:, 0:HALF]
            found.append(wide.reshape(SEQ * HALF, wide.shape[2]) + bias)
        return found

    pairs = ((keys_a, values_a), (keys_b, values_b))
    group = SEQ * HALF
    mine = slot_group[slot]

    def pair(i):
        keys, values = pairs[i % 2]
        for odd in (0, 1):
            b = lax.rem(slot + offset(odd, i) + 1, SLOTS)
            keep = jnp.full((1, HD), group_mask[mine, slot_group[b]], jnp.int32).astype(F32)
            for half, t in enumerate(tokens(odd, i, a_kv[odd, i], b_kv[odd, i][0:1])):
                first = (2 * odd + half) * group
                rows = slice(first, first + group)
                keys[rows, :] = unit(t[:, 0:HD]).astype(BF16)
                values[rows, 0:HD] = (t[:, HD : 2 * HD] * keep).astype(BF16)
                values[rows, HD : 2 * HD] = jnp.broadcast_to(keep, (group, HD)).astype(BF16)

    def attend(i):
        keys, values = pairs[i % 2]
        scores = lax.dot_general(q_ref[...], keys[...], NT, preferred_element_type=F32)
        probs = jnp.exp2(scores).astype(BF16)
        total[...] += jnp.dot(probs, values[...], preferred_element_type=F32)

    total[...] = jnp.zeros_like(total)
    def queries():
        scale = 1.0 / (math.sqrt(HD) * math.log(2.0))
        for half, t in enumerate(tokens(1, 0, a_q.astype(BF16), b_q)):
            q_ref[half * group : half * group + group, :] = (unit(t) * scale).astype(BF16)

    def run(what, first, last):
        for i in range(first, last + 1):
            what(i)

    steps = {
        "mf": m.first,
        "ms": m.second,
        "mh": m.fourth,
        "xf": x.first,
        "xs": x.second,
        "xt": x.third,
        "xh": x.fourth,
        "B": build,
        "P": pair,
        "A": attend,
    }
    for what, i in ORDER:
        if what == "Q":
            queries()
        else:
            steps[what](i)
    for p in range(SEQ):
        found = []
        for half in range(2):
            rows = slice(half * group + p * HALF, half * group + p * HALF + HALF)
            found.append(total[rows, 0:HD] / total[rows, HD : 2 * HD])
        attn[p * TOK : p * TOK + TOK, :] = jnp.concatenate(found, axis=0).astype(attn.dtype)
    attn_copy = pltpu.make_async_copy(attn, attn_out, local_sem.at[1])
    attn_copy.start()
    for copy in sends:
        copy.wait_send()
    m.finish()
    x.finish()
    stepped_copy.wait()
    attn_copy.wait()


def spread_sems():
    dma = pltpu.SemaphoreType.DMA
    return [dma((SLOTS,)) for _ in range(8)]


def local(
    hidden,
    final_mod,
    head_weight,
    latents,
    fresh_noise,
    step_index,
    slot_group,
    group_mask,
    patch_weight,
    block_mod,
    qkv_weight,
):
    hbm = pl.BlockSpec(memory_space=pl.ANY)
    dma = pltpu.SemaphoreType.DMA
    vmem = pltpu.VMEM
    smem = pltpu.SMEM
    stepped_t, attn = pl.pallas_call(
        kernel,
        out_shape=(
            jax.ShapeDtypeStruct((PATCH, TOK), F32),
            jax.ShapeDtypeStruct((SEQ * TOK, HD), BF16),
        ),
        in_specs=[hbm] * 11,
        out_specs=(hbm, hbm),
        scratch_shapes=[
            vmem((TOK, D // HEADS), BF16),
            vmem((1, 2, D // HEADS), F32),
            vmem((PATCH, D // HEADS), F32),
            vmem((PATCH, TOK), F32),
            vmem((PATCH, TOK), F32),
            smem((SLOTS,), jnp.int32),
            smem((SLOTS,), jnp.int32),
            smem((SLOTS, SLOTS), jnp.int32),
            vmem((PATCH, D), BF16),
            vmem((1, 2, D), F32),
            vmem((D, HD), BF16),
            vmem((D, 2 * HD), BF16),
            vmem((PATCH, TOK), F32),
            vmem((SEQ * TOK, HD), BF16),
            vmem((2, PAIRS, SEQ, XROWS, 128), BF16),
            vmem((2, PAIRS, SEQ, MROWS, 128), BF16),
            vmem((XROWS, 128), F32),
            vmem((HEADS - 1, XROWS, 128), F32),
            vmem((PATCH, D), F32),
            vmem((4 * (PATCH + MROWS), D), BF16),
            vmem((2, PAIRS, PATCH, 2 * HD), BF16),
            vmem((2, PAIRS, 8, 2 * HD), F32),
            vmem((SEQ * TOK, HD), BF16),
            vmem((KEYS, HD), BF16),
            vmem((KEYS, 2 * HD), BF16),
            vmem((KEYS, HD), BF16),
            vmem((KEYS, 2 * HD), BF16),
            vmem((SEQ * TOK, 2 * HD), F32),
            dma((13,)),
            dma((HEADS - 1,)),
            dma((HEADS - 1,)),
        ]
        + spread_sems()
        + spread_sems(),
        compiler_params=pltpu.CompilerParams(
            collective_id=0, has_side_effects=True, vmem_limit_bytes=56 * 2**20
        ),
        name="window",
    )(
        hidden,
        final_mod,
        head_weight.T,
        latents.T,
        fresh_noise.T,
        step_index,
        slot_group,
        group_mask,
        patch_weight,
        block_mod,
        jnp.transpose(qkv_weight, (1, 0, 2)),
    )
    return stepped_t.T, attn


def solution(mesh):
    in_specs = (
        P(("slot", "seq"), "head"),
        P("slot", None, "head"),
        P("head", None),
        P(("slot", "seq"), None),
        P("seq", None),
        P(),
        P(),
        P(),
        P(),
        P("slot", None, None),
        P(None, None, ("seq", "head")),
    )
    out_specs = (P(("slot", "seq"), None), P("slot", ("seq", "head")))
    return jax.shard_map(local, mesh=mesh, in_specs=in_specs, out_specs=out_specs, check_vma=False)
```

```python
import math

import jax
import jax.numpy as jnp
from jax import lax
from jax.experimental import pallas as pl
from jax.experimental.pallas import tpu as pltpu
from jax.sharding import PartitionSpec as P

D = 5120
HD = 128
STEPS = 48
PATCH = 64
SLOTS = 16
SEQ = 8
HEADS = 4
CHUNKS = D // 128
TOK = 80
HALF = 40
XROWS = 48
MROWS = 16
FEAT = D // SEQ
EPS = 1e-06
MESH = pl.DeviceIdType.MESH
HIGHEST = lax.Precision.HIGHEST
F32 = jnp.float32
BF16 = jnp.bfloat16
NT = (((1,), (1,)), ((), ()))
PAIRS = SLOTS // 2
ROW = SEQ // 2
STEPS_EACH = 2
RELAYED = 4
MOD_RELAYED = 0
ORDER = (
    ("mf", 0), ("mf", 1), ("mf", 2), ("xf", 0), ("ms", 0), ("mf", 3), ("xf", 1), ("ms", 1), ("mh", 0),
    ("B", 0), ("xf", 2), ("ms", 2), ("mh", 1), ("xs", 0), ("B", 1), ("xf", 3), ("xs", 1), ("ms", 3),
    ("mh", 2), ("B", 2), ("xs", 2), ("mh", 3), ("xt", 0), ("B", 3), ("xs", 3), ("xt", 1), ("xh", 0),
    ("Q", 0), ("P", 0), ("P", 1), ("A", 0), ("xt", 2), ("xh", 1), ("P", 2), ("A", 1), ("xt", 3),
    ("P", 3), ("A", 2), ("xh", 2), ("P", 4), ("A", 3), ("P", 5), ("A", 4), ("xh", 3), ("P", 6),
    ("A", 5), ("P", 7), ("A", 6), ("A", 7),
)
PARTS = FEAT // 128
KEYS = 2 * SEQ * TOK


def remote(src, dst, send_sem, recv_sem, device_id):
    return pltpu.make_async_remote_copy(
        src_ref=src,
        dst_ref=dst,
        send_sem=send_sem,
        recv_sem=recv_sem,
        device_id=device_id,
        device_id_type=MESH,
    )


def offset(odd, step):
    if odd:
        return step if step % 2 else SLOTS - 1 - step
    return (step + 1 if step % 2 else SLOTS - step) % SLOTS


class Spread:
    def __init__(self, buf, ahead, relayed, sems):
        self.buf = buf
        self.relayed = relayed
        self.zs, self.zr, self.qs, self.qr, self.ys, self.yr, self.cs, self.cr = sems
        self.slot = lax.axis_index("slot")
        self.seq = lax.axis_index("seq")
        self.head = lax.axis_index("head")
        self.core = lax.rem(self.head, 2)
        self.own = lax.rem(self.slot, 2) == self.core
        self.mine = jnp.where(self.own, 0, 1)
        self.other_core = self.head + 1 - 2 * self.core
        self.low = self.seq // ROW
        self.at = lax.rem(self.seq, ROW)
        self.place = {}
        for odd in (0, 1):
            for step in range(PAIRS):
                far = (offset(1 - odd, step) + 1) % SLOTS if ahead else offset(odd, step)
                self.place[far] = (odd, step)

    def slot_copy(self, k):
        odd, step = self.place[SLOTS - k]
        return remote(
            self.buf.at[0, 0, self.seq],
            self.buf.at[odd, step, self.seq],
            self.zs.at[k],
            self.zr.at[step],
            {"slot": lax.rem(self.slot + k, SLOTS)},
        )

    def slot_send(self):
        @pl.when(self.own)
        def _():
            for k in range(1, SLOTS):
                self.slot_copy(k // 2 if k % 2 == 0 else SLOTS - (k + 1) // 2).start()

    def slot_wait(self, step):
        def wait():
            block = self.buf.at[self.mine, step, self.seq]
            remote(block, block, self.zs.at[0], self.zr.at[step], {"slot": self.slot}).wait_recv()

        if step:
            wait()
        else:
            pl.when(jnp.logical_not(self.own))(wait)

    def blocks(self, g, seqs, mine=True):
        steps = pl.ds(g * STEPS_EACH, STEPS_EACH)
        return self.buf.at[self.mine if mine else 1 - self.mine, steps, seqs]

    def copy(self, blocks, send, recv, g, device_id):
        return remote(blocks, blocks, send.at[g], recv.at[g], device_id)

    def row_copy(self, g, k):
        relay = g < self.relayed
        to = self.low * ROW + lax.rem(self.at + k, ROW) if relay else lax.rem(self.seq + k, SEQ)
        return self.copy(self.blocks(g, self.seq), self.qs, self.qr, g, {"seq": to})

    def row_all(self, g):
        count = (ROW if g < self.relayed else SEQ) - 1
        return self.copy(self.blocks(g, pl.ds(0, count)), self.qs, self.qr, g, {"seq": self.seq})

    def side_copy(self, g):
        head = lax.rem(self.head + 2 * (g % 2), HEADS)
        seq = (1 - self.low) * ROW + self.at
        near = self.blocks(g, pl.ds(self.low * ROW, ROW))
        return self.copy(near, self.ys, self.yr, g, {"seq": seq, "head": head})

    def core_copy(self, g, seqs, mine=True):
        return self.copy(self.blocks(g, seqs, mine), self.cs, self.cr, g, {"head": self.other_core})

    def first(self, g):
        for step in range(g * STEPS_EACH, (g + 1) * STEPS_EACH):
            self.slot_wait(step)
        for k in range(1, ROW if g < self.relayed else SEQ):
            self.row_copy(g, k).start()

    def second(self, g):
        self.row_all(g).wait_recv()
        if g < self.relayed:
            self.side_copy(g).start()
            self.core_copy(g, pl.ds(self.low * ROW, ROW)).start()
        else:
            self.core_copy(g, pl.ds(0, SEQ)).start()

    def third(self, g):
        if g < self.relayed:
            self.side_copy(g).wait_recv()
            self.core_copy(g, pl.ds((1 - self.low) * ROW, ROW)).start()

    def fourth(self, g):
        self.core_copy(g, pl.ds(0, SEQ), False).wait_recv()

    def finish(self):
        @pl.when(self.own)
        def _():
            for k in range(1, SLOTS):
                self.slot_copy(k).wait_send()

        for g in range(PAIRS // STEPS_EACH):
            self.row_all(g).wait_send()
            if g < self.relayed:
                self.side_copy(g).wait_send()
            self.core_copy(g, pl.ds(0, SEQ)).wait_send()


def split(value, count):
    found = []
    for _ in range(count):
        part = value.astype(BF16)
        found.append(part)
        value = value - part.astype(F32)
    return found


def partial_velocity(hidden, final_mod, head_t, msg):
    h = hidden[...]
    wide = h.astype(F32)
    mean = jnp.mean(wide, axis=1, keepdims=True)
    centred = wide - mean
    spread = jnp.sum(centred * centred, axis=1, keepdims=True)
    gained = head_t[...] * (1.0 + final_mod[0, 0:1, :])
    gain_sum = jnp.sum(gained, axis=1, keepdims=True)
    shift_sum = jnp.sum(head_t[...] * final_mod[0, 1:2, :], axis=1, keepdims=True)
    stack = jnp.concatenate(split(gained, 3), axis=0)
    parts = lax.dot_general(h, stack, NT, preferred_element_type=F32)
    part = parts[:, 0:PATCH] + parts[:, PATCH : 2 * PATCH] + parts[:, 2 * PATCH : 3 * PATCH]
    lane = lax.broadcasted_iota(jnp.int32, (TOK, 128), 1)
    pad = jnp.zeros((TOK - PATCH, 1), F32)
    gain_sum = jnp.concatenate([gain_sum, pad], axis=0)
    shift_sum = jnp.concatenate([shift_sum, pad], axis=0)
    stats = jnp.where(lane == 0, mean, jnp.where(lane == 1, spread, 0.0))
    stats = jnp.where(lane == 2, gain_sum, jnp.where(lane == 3, shift_sum, stats))
    stats = jnp.transpose(jnp.concatenate([stats, jnp.zeros((128 - TOK, 128), F32)], axis=0))
    msg[0:HALF, :] = jnp.concatenate([part[0:HALF], part[HALF:TOK]], axis=1)
    msg[HALF:XROWS, :] = stats[0:8]


def whole_velocity(parts, count):
    total = sum(parts)
    mean = total[HALF : HALF + 1] / len(parts)
    spread = total[HALF + 1 : HALF + 2]
    for p in parts:
        off = p[HALF : HALF + 1] - mean
        spread = spread + count * off * off
    scale = lax.rsqrt(spread / (count * len(parts)) + EPS)
    turned = jnp.transpose(jnp.concatenate([mean, scale, jnp.zeros((126, 128), F32)], axis=0))[0:TOK]
    gain_row = total[HALF + 2 : HALF + 3, 0:PATCH]
    shift_row = total[HALF + 3 : HALF + 4, 0:PATCH]
    product = jnp.concatenate([total[0:HALF, 0:PATCH], total[0:HALF, PATCH:128]], axis=0)
    return (product - turned[:, 0:1] * gain_row) * turned[:, 1:2] + shift_row


def sigma_of(level):
    ratio = jnp.full((1, PATCH), level, jnp.int32).astype(F32) / STEPS
    return 5.0 * ratio / (1.0 + 4.0 * ratio)


def unit(block):
    return block * lax.rsqrt(jnp.mean(block * block, axis=1, keepdims=True) + EPS)


def kernel(
    hidden_in,
    final_mod_in,
    head_in,
    latents_in,
    noise_in,
    step_in,
    group_in,
    mask_in,
    patch_in,
    block_in,
    qkv_in,
    stepped_out,
    attn_out,
    hidden,
    final_mod,
    head_t,
    latents_t,
    noise_t,
    step_index,
    slot_group,
    group_mask,
    patch_weight,
    block_mod,
    q_weight,
    kv_weight,
    stepped_t,
    attn,
    xall,
    mall,
    msg,
    got,
    centred,
    lhs,
    a_kv,
    b_kv,
    q_ref,
    keys_a,
    values_a,
    keys_b,
    values_b,
    total,
    local_sem,
    ps,
    pr,
    *sems,
):
    x = Spread(xall, False, RELAYED, sems[:8])
    m = Spread(mall, True, MOD_RELAYED, sems[8:])
    slot, seq, head = x.slot, x.seq, x.head
    loads = [
        pltpu.make_async_copy(src, dst, local_sem.at[i])
        for i, (src, dst) in enumerate(
            (
                (hidden_in, hidden),
                (final_mod_in, final_mod),
                (head_in, head_t),
                (block_in, block_mod),
                (patch_in, patch_weight),
                (latents_in, latents_t),
                (noise_in, noise_t),
                (step_in, step_index),
                (group_in, slot_group),
                (mask_in, group_mask),
                (qkv_in.at[0], q_weight),
                (qkv_in.at[1], kv_weight.at[:, 0:HD]),
                (qkv_in.at[2], kv_weight.at[:, HD : 2 * HD]),
            )
        )
    ]
    for copy in loads:
        copy.start()
    barrier = pltpu.get_barrier_semaphore()

    def greet(device_id):
        pl.semaphore_signal(barrier, inc=1, device_id=device_id, device_id_type=MESH)

    for k in range(1, SLOTS):
        greet({"slot": lax.rem(slot + k, SLOTS)})
    for k in range(1, HEADS):
        greet({"head": lax.rem(head + k, HEADS)})
    for k in range(1, SEQ):
        greet({"seq": lax.rem(seq + k, SEQ)})
    side = (1 - x.low) * ROW + x.at
    greet({"seq": side, "head": lax.rem(head + 2, HEADS)})

    for copy in loads[:4]:
        copy.wait()
    partial_velocity(hidden, final_mod, head_t, msg)
    sub = lax.broadcasted_iota(jnp.int32, (MROWS, 128), 0)

    @pl.when(x.own)
    def _():
        start = pl.multiple_of(seq * FEAT, 128)
        gain = 1.0 + block_mod[0, 0:1, pl.ds(start, FEAT)]
        high, low = split(block_mod[0, 1:2, pl.ds(start, FEAT)], 2)
        rows = []
        for row in (gain, high.astype(F32), low.astype(F32)):
            rows += [row[:, 128 * r : 128 * r + 128] for r in range(PARTS)]
        rows += [jnp.zeros((1, 128), F32)]
        mall[0, 0, seq] = jnp.concatenate(rows, axis=0).astype(BF16)

    pl.semaphore_wait(barrier, SLOTS + HEADS + SEQ - 3 + 1)
    sends = [
        remote(msg, got.at[k - 1], ps.at[k - 1], pr.at[k - 1], {"head": lax.rem(head + k, HEADS)})
        for k in range(1, HEADS)
    ]
    for copy in sends:
        copy.start()
    m.slot_send()

    for copy in loads[4:]:
        copy.wait()
    weight = patch_weight[...]
    gram = lax.dot_general(weight, weight, NT, preferred_element_type=F32) / D
    ones = jnp.ones((16, D), BF16)
    mean_row = lax.dot_general(ones, weight, NT, preferred_element_type=F32)[0:8] / D
    mean_outer = lax.dot_general(
        mean_row, mean_row, (((0,), (0,)), ((), ())), precision=HIGHEST, preferred_element_type=F32
    ) / 8.0
    gram = gram - mean_outer
    latents = jnp.transpose(latents_t[...])
    noise = jnp.transpose(noise_t[...])
    now = step_index[slot]
    later = jnp.where(slot == SLOTS - 1, 0, step_index[jnp.minimum(slot + 1, SLOTS - 1)])
    delta = sigma_of(later) - sigma_of(now)

    wide = weight.astype(F32)
    centred[...] = wide - jnp.mean(wide, axis=1, keepdims=True)
    own_rows = PATCH + MROWS
    for c in range(CHUNKS):
        lanes = slice(128 * c, 128 * c + 128)
        gain = 1.0 + block_mod[0, 0:1, lanes]
        high, low = split(block_mod[0, 1:2, lanes], 2)
        lhs[0:PATCH, lanes] = (centred[:, lanes] * gain).astype(BF16)
        shifts = jnp.where(sub == 0, high.astype(F32), jnp.where(sub == 1, low.astype(F32), 0.0))
        lhs[PATCH:own_rows, lanes] = shifts.astype(BF16)
    found = jnp.dot(lhs[0:own_rows, :], q_weight[...], preferred_element_type=F32)
    a_q = found[0:PATCH]
    b_q = jnp.sum(found[PATCH:own_rows], axis=0, keepdims=True)

    for copy in sends:
        copy.wait_recv()
    velocity = whole_velocity([msg[...]] + [got[k] for k in range(HEADS - 1)], D // HEADS)
    stepped = latents + delta * velocity
    shifted = jnp.where(slot == SLOTS - 1, noise, stepped).astype(BF16).astype(F32)
    projected = jnp.dot(shifted, gram, precision=HIGHEST, preferred_element_type=F32)
    spread = jnp.sum(projected * shifted, axis=1, keepdims=True)
    scaled = shifted * lax.rsqrt(jnp.maximum(spread, 0.0) + EPS)
    block = jnp.concatenate([scaled[0:HALF], scaled[HALF:TOK]], axis=1)
    block = jnp.concatenate([block, jnp.zeros((XROWS - HALF, 128), F32)], axis=0).astype(BF16)

    @pl.when(x.own)
    def _():
        xall[0, 0, seq] = block

    x.slot_send()
    stepped_t[...] = jnp.transpose(stepped)
    stepped_copy = pltpu.make_async_copy(stepped_t, stepped_out, local_sem.at[0])
    stepped_copy.start()

    def build(k):
        steps = [(odd, 2 * k + e) for e in range(2) for odd in (0, 1)]
        for at, (odd, step) in enumerate(steps):
            first = at * own_rows
            for p in range(SEQ):
                mods = mall[1 - odd, step, p].astype(F32)
                for r in range(PARTS):
                    lanes = slice(p * FEAT + 128 * r, p * FEAT + 128 * r + 128)
                    lhs[first : first + PATCH, lanes] = (centred[:, lanes] * mods[r : r + 1]).astype(BF16)
                    kept = jnp.where((sub == PARTS + r) | (sub == 2 * PARTS + r), mods, 0.0)
                    lhs[first + PATCH : first + own_rows, lanes] = kept.astype(BF16)

        found = jnp.dot(lhs[...], kv_weight[...], preferred_element_type=F32)
        for at, (odd, step) in enumerate(steps):
            first = at * own_rows
            bias = jnp.sum(found[first + PATCH : first + own_rows], axis=0, keepdims=True)
            a_kv[odd, step] = found[first : first + PATCH].astype(BF16)
            b_kv[odd, step] = jnp.broadcast_to(bias, (8, 2 * HD))

    def tokens(odd, step, matrix, bias):
        blocks = xall[odd, step].reshape(SEQ * XROWS, 128)
        zero = jnp.zeros_like(matrix)
        found = []
        for pair in ([matrix, zero], [zero, matrix]):
            wide = jnp.dot(blocks, jnp.concatenate(pair, axis=0), preferred_element_type=F32)
            wide = wide.reshape(SEQ, XROWS, wide.shape[1])[:, 0:HALF]
            found.append(wide.reshape(SEQ * HALF, wide.shape[2]) + bias)
        return found

    pairs = ((keys_a, values_a), (keys_b, values_b))
    group = SEQ * HALF
    mine = slot_group[slot]

    def pair(i):
        keys, values = pairs[i % 2]
        for odd in (0, 1):
            b = lax.rem(slot + offset(odd, i) + 1, SLOTS)
            keep = jnp.full((1, HD), group_mask[mine, slot_group[b]], jnp.int32).astype(F32)
            for half, t in enumerate(tokens(odd, i, a_kv[odd, i], b_kv[odd, i][0:1])):
                first = (2 * odd + half) * group
                rows = slice(first, first + group)
                keys[rows, :] = unit(t[:, 0:HD]).astype(BF16)
                values[rows, 0:HD] = (t[:, HD : 2 * HD] * keep).astype(BF16)
                values[rows, HD : 2 * HD] = jnp.broadcast_to(keep, (group, HD)).astype(BF16)

    def attend(i):
        keys, values = pairs[i % 2]
        scores = lax.dot_general(q_ref[...], keys[...], NT, preferred_element_type=F32)
        probs = jnp.exp2(scores).astype(BF16)
        total[...] += jnp.dot(probs, values[...], preferred_element_type=F32)

    total[...] = jnp.zeros_like(total)
    def queries():
        scale = 1.0 / (math.sqrt(HD) * math.log(2.0))
        for half, t in enumerate(tokens(1, 0, a_q.astype(BF16), b_q)):
            q_ref[half * group : half * group + group, :] = (unit(t) * scale).astype(BF16)

    def run(what, first, last):
        for i in range(first, last + 1):
            what(i)

    steps = {
        "mf": m.first,
        "ms": m.second,
        "mh": m.fourth,
        "xf": x.first,
        "xs": x.second,
        "xt": x.third,
        "xh": x.fourth,
        "B": build,
        "P": pair,
        "A": attend,
    }
    for what, i in ORDER:
        if what == "Q":
            queries()
        else:
            steps[what](i)
    for p in range(SEQ):
        found = []
        for half in range(2):
            rows = slice(half * group + p * HALF, half * group + p * HALF + HALF)
            found.append(total[rows, 0:HD] / total[rows, HD : 2 * HD])
        attn[p * TOK : p * TOK + TOK, :] = jnp.concatenate(found, axis=0).astype(attn.dtype)
    attn_copy = pltpu.make_async_copy(attn, attn_out, local_sem.at[1])
    attn_copy.start()
    for copy in sends:
        copy.wait_send()
    m.finish()
    x.finish()
    stepped_copy.wait()
    attn_copy.wait()


def spread_sems():
    dma = pltpu.SemaphoreType.DMA
    return [dma((SLOTS,)) for _ in range(8)]


def local(
    hidden,
    final_mod,
    head_weight,
    latents,
    fresh_noise,
    step_index,
    slot_group,
    group_mask,
    patch_weight,
    block_mod,
    qkv_weight,
):
    hbm = pl.BlockSpec(memory_space=pl.ANY)
    dma = pltpu.SemaphoreType.DMA
    vmem = pltpu.VMEM
    smem = pltpu.SMEM
    stepped_t, attn = pl.pallas_call(
        kernel,
        out_shape=(
            jax.ShapeDtypeStruct((PATCH, TOK), F32),
            jax.ShapeDtypeStruct((SEQ * TOK, HD), BF16),
        ),
        in_specs=[hbm] * 11,
        out_specs=(hbm, hbm),
        scratch_shapes=[
            vmem((TOK, D // HEADS), BF16),
            vmem((1, 2, D // HEADS), F32),
            vmem((PATCH, D // HEADS), F32),
            vmem((PATCH, TOK), F32),
            vmem((PATCH, TOK), F32),
            smem((SLOTS,), jnp.int32),
            smem((SLOTS,), jnp.int32),
            smem((SLOTS, SLOTS), jnp.int32),
            vmem((PATCH, D), BF16),
            vmem((1, 2, D), F32),
            vmem((D, HD), BF16),
            vmem((D, 2 * HD), BF16),
            vmem((PATCH, TOK), F32),
            vmem((SEQ * TOK, HD), BF16),
            vmem((2, PAIRS, SEQ, XROWS, 128), BF16),
            vmem((2, PAIRS, SEQ, MROWS, 128), BF16),
            vmem((XROWS, 128), F32),
            vmem((HEADS - 1, XROWS, 128), F32),
            vmem((PATCH, D), F32),
            vmem((4 * (PATCH + MROWS), D), BF16),
            vmem((2, PAIRS, PATCH, 2 * HD), BF16),
            vmem((2, PAIRS, 8, 2 * HD), F32),
            vmem((SEQ * TOK, HD), BF16),
            vmem((KEYS, HD), BF16),
            vmem((KEYS, 2 * HD), BF16),
            vmem((KEYS, HD), BF16),
            vmem((KEYS, 2 * HD), BF16),
            vmem((SEQ * TOK, 2 * HD), F32),
            dma((13,)),
            dma((HEADS - 1,)),
            dma((HEADS - 1,)),
        ]
        + spread_sems()
        + spread_sems(),
        compiler_params=pltpu.CompilerParams(
            collective_id=0, has_side_effects=True, vmem_limit_bytes=56 * 2**20
        ),
        name="window",
    )(
        hidden,
        final_mod,
        head_weight.T,
        latents.T,
        fresh_noise.T,
        step_index,
        slot_group,
        group_mask,
        patch_weight,
        block_mod,
        jnp.transpose(qkv_weight, (1, 0, 2)),
    )
    return stepped_t.T, attn


def solution(mesh):
    in_specs = (
        P(("slot", "seq"), "head"),
        P("slot", None, "head"),
        P("head", None),
        P(("slot", "seq"), None),
        P("seq", None),
        P(),
        P(),
        P(),
        P(),
        P("slot", None, None),
        P(None, None, ("seq", "head")),
    )
    out_specs = (P(("slot", "seq"), None), P("slot", ("seq", "head")))
    return jax.shard_map(local, mesh=mesh, in_specs=in_specs, out_specs=out_specs, check_vma=False)
```
